256 devices in a mesh: mem: 8 (over y, core), patch: 32 (over x, z).
Axes of the slice: x: 4, y: 4, z: 8, core: 2. Of those that a mesh axis runs over, the one named last changes fastest.
Arguments:
- mesh_latent: bfloat16 [8, 16384, 512], P('mem', 'patch'), may hold values from -6 to 6
- edge_latent: bfloat16 [32768, 512], P('patch'), may hold values from -6 to 6
- grid_edge_latent: bfloat16 [49152, 512], P('patch'), may hold values from -6 to 6
- edge_inner: bfloat16 [1536, 512], replicated, may hold values from -0.15625 to 0.15625
- edge_outer: bfloat16 [512, 512], replicated, may hold values from -0.25 to 0.25
- node_inner: bfloat16 [1024, 512], replicated, may hold values from -0.1875 to 0.1875
- node_outer: bfloat16 [512, 512], replicated, may hold values from -0.25 to 0.25
- grid_inner: bfloat16 [1024, 512], replicated, may hold values from -0.1875 to 0.1875
- grid_outer: bfloat16 [512, 512], replicated, may hold values from -0.25 to 0.25
- out_weight: bfloat16 [87, 512], replicated, may hold values from -0.25 to 0.25
- prior_state: float32 [87, 16384], P(None, 'patch'), may hold values from -6 to 6
- target: float32 [87, 16384], P(None, 'patch'), may hold values from -6 to 6
- channel_weight: float32 [87], replicated, may hold values from 0.2 to 2
- area_weight: float32 [16384], P('patch'), may hold values from 0.2 to 2
- send_rows: int32 [32, 2, 96], P('patch'), may hold values from 0 to 511
- edge_senders: int32 [32768], P('patch'), may hold values from 0 to 703, as said below
- edge_receivers: int32 [32768], P('patch'), may hold values from 0 to 511
- edge_count: int32 [32], P('patch'), may hold values from 256 to 1024, as said below
- grid_senders: int32 [49152], P('patch'), may hold values from 0 to 703, as said below
Outputs:
- crps_gradient: float32 [8, 87, 16384], P('mem', None, 'patch')
The draws below stay inside these ranges and needn't reach their ends.
Inputs may be any that keep to these rules, and one draw needn't show every extreme that they name: `edge_senders`: values below 512 name a row of the band itself, values from 512 to 607 a row received from the previous band, larger values a row received from the next band; the first band names none of the second kind and the last band none of the third. `grid_senders`: as for edge_senders: own rows, rows from the previous band, rows from the next band; the first and last bands name only bands that exist. The live slots of a band are its first edge_count slots; some band has all 1024 slots live.
All inputs are finite; a program needn't handle non-finite values.
Results may differ from the reference program's by a relative error of at most 0.023.
Values may be sent and summed in bfloat16 or wider, within the bound.
A program may use at most 64 MiB of HBM per device.

```python
import math
import jax
import jax.numpy as jnp
from jax import lax

D = 512
C = 87
NODE_DEV = 512
EDGE_DEV = 1024
DEC_DEV = 1536
HALO = 96
MEMBERS = 8
NODES = 16384
EDGES = 32768
DEC_EDGES = 49152
GRID = 16384
N_PATCH = 32


def pick_senders(key, slots):
    region = jax.random.randint(jax.random.fold_in(key, 1), (N_PATCH, slots), 0, 10)
    own_rows = jax.random.randint(jax.random.fold_in(key, 2), (N_PATCH, slots), 0, NODE_DEV)
    halo_rows = jax.random.randint(jax.random.fold_in(key, 3), (N_PATCH, slots), 0, HALO)
    patch_index = jnp.arange(N_PATCH)[:, None]
    lower = (region >= 6) & (region < 8) & (patch_index > 0)
    upper = (region >= 8) & (patch_index < N_PATCH - 1)
    chosen = jnp.where(lower, NODE_DEV + halo_rows, jnp.where(upper, NODE_DEV + HALO + halo_rows, own_rows))
    return chosen.reshape(-1).astype(jnp.int32)


def draw_edge_senders(key, part):
    return pick_senders(jax.random.fold_in(key, 11), EDGE_DEV)


def draw_grid_senders(key, part):
    return pick_senders(jax.random.fold_in(key, 12), DEC_DEV)


def draw_edge_count(key, part):
    counts = jax.random.randint(jax.random.fold_in(key, 21), (N_PATCH,), EDGE_DEV // 4, EDGE_DEV + 1)
    fullest = jax.random.randint(jax.random.fold_in(key, 22), (), 0, N_PATCH)
    return counts.at[fullest].set(EDGE_DEV).astype(jnp.int32)


def place_ends(array, own_key, smallest, largest):
    longest = array.shape.index(max(array.shape))
    spots = []
    for shift in (0, 1):
        where = [jax.random.randint(jax.random.fold_in(own_key, axis), (), 0, length) for axis, length in enumerate(array.shape)]
        where[longest] = (where[longest] + shift) % array.shape[longest]
        spots.append(tuple(where))
    return array.at[spots[0]].set(smallest).at[spots[1]].set(largest)


def block_scale(stream_key, dims, cuts, smallest, top_value):
    gain = 1.0
    for position, blocks in cuts:
        draws = jax.random.uniform(jax.random.fold_in(jax.random.fold_in(stream_key, 6), position), (blocks,), jnp.float32, smallest / len(cuts), top_value / len(cuts))
        gain = gain * jnp.repeat(jnp.exp(draws), dims[position] // blocks).reshape((-1,) + (1,) * (len(dims) - 1 - position))
    return gain


def bell_draw(stream_key, extent, scale, bound, cuts=(), kind=jnp.bfloat16):
    loudness = block_scale(stream_key, extent, cuts, -0.22, 0.18) if cuts else 1.0
    values = jax.random.normal(stream_key, extent, jnp.float32) * scale * loudness
    return jnp.minimum(jnp.maximum(values, -bound), bound).astype(kind)


def setup_inputs(seed: int = 0) -> dict:
    streams_of = jax.random.split(jax.random.key(seed), 20)
    return {
        "mesh_latent": bell_draw(streams_of[0], (MEMBERS, NODES, D), 1.0, 6.0, ((0, 8), (1, 32))),
        "edge_latent": bell_draw(streams_of[1], (EDGES, D), 1.0, 6.0, ((0, 32),)),
        "grid_edge_latent": bell_draw(streams_of[2], (DEC_EDGES, D), 1.0, 6.0, ((0, 32),)),
        "edge_inner": bell_draw(streams_of[3], (3 * D, D), (3 * D) ** -0.5, 0.15625),
        "edge_outer": bell_draw(streams_of[4], (D, D), D ** -0.5, 0.25),
        "node_inner": bell_draw(streams_of[5], (2 * D, D), (2 * D) ** -0.5, 0.1875),
        "node_outer": bell_draw(streams_of[6], (D, D), D ** -0.5, 0.25),
        "grid_inner": bell_draw(streams_of[7], (2 * D, D), (2 * D) ** -0.5, 0.1875),
        "grid_outer": bell_draw(streams_of[8], (D, D), D ** -0.5, 0.25),
        "out_weight": bell_draw(streams_of[9], (C, D), D ** -0.5, 0.25),
        "prior_state": bell_draw(streams_of[10], (C, GRID), 1.0, 6.0, ((1, 32),), jnp.float32),
        "target": bell_draw(streams_of[11], (C, GRID), 1.0, 6.0, ((1, 32),), jnp.float32),
        "channel_weight": jnp.clip(jnp.exp(jax.random.uniform(streams_of[12], (C,), jnp.float32, math.log(0.2), math.log(2.0))), 0.2, 2.0),
        "area_weight": jnp.clip(jnp.exp(math.log(2.0) - 2.3025851 * jax.random.uniform(streams_of[13], (GRID,), jnp.float32) ** block_scale(streams_of[13], (GRID,), ((0, 32),), -0.2, 0.2)), 0.2, 2.0),
        "send_rows": place_ends(jax.random.randint(streams_of[14], (N_PATCH, 2, HALO), 0, NODE_DEV), jax.random.fold_in(streams_of[14], 1), 0, NODE_DEV - 1).astype(jnp.int32),
        "edge_senders": draw_edge_senders(jax.random.fold_in(streams_of[19], 71), 0),
        "edge_receivers": place_ends(jax.random.randint(streams_of[16], (EDGES,), 0, NODE_DEV), jax.random.fold_in(streams_of[16], 1), 0, NODE_DEV - 1).astype(jnp.int32),
        "edge_count": draw_edge_count(jax.random.fold_in(streams_of[19], 71), 0),
        "grid_senders": draw_grid_senders(jax.random.fold_in(streams_of[19], 71), 0),
    }


epsilon = 1e-05
smooth = 0.25

def layer_norm(values):
    average = lax.optimization_barrier(jnp.mean(values, -1, keepdims=True))
    centred = values - average
    spread = lax.optimization_barrier(jnp.mean(centred * centred, -1, keepdims=True))
    return centred / jnp.sqrt(spread + epsilon)

def network(inputs, inner_weight, outer_weight):
    inner = jax.nn.silu(jnp.dot(inputs, inner_weight, preferred_element_type=jnp.float32)).astype(jnp.bfloat16)
    return layer_norm(jnp.dot(inner, outer_weight, preferred_element_type=jnp.float32))

def smooth_slope(values):
    return values / jnp.sqrt(values * values + smooth * smooth)

def take_rows(table, rows):
    return table[rows]

def reference(mesh_latent, edge_latent, grid_edge_latent, edge_inner, edge_outer, node_inner, node_outer, grid_inner, grid_outer, out_weight, prior_state, target, channel_weight, area_weight, send_rows, edge_senders, edge_receivers, edge_count, grid_senders):
    gather_rows = jax.vmap(take_rows)

    def extend(latent):
        upward = gather_rows(latent, send_rows[:, 0])
        downward = gather_rows(latent, send_rows[:, 1])
        blank = jnp.zeros((1, HALO, D), latent.dtype)
        lower = jnp.concatenate([blank, upward[:-1]], 0)
        upper = jnp.concatenate([downward[1:], blank], 0)
        return jnp.concatenate([latent, lower, upper], 1)
    senders = edge_senders.reshape(N_PATCH, EDGE_DEV)
    receivers = edge_receivers.reshape(N_PATCH, EDGE_DEV)
    grid_rows = grid_senders.reshape(N_PATCH, DEC_DEV)
    live_slots = jnp.arange(EDGE_DEV, dtype=jnp.int32)[None, :] < edge_count[:, None]

    def add_rows(values, rows):
        return jax.ops.segment_sum(values, rows, NODE_DEV)

    def member(latent):
        extended = extend(latent)
        inputs = jnp.concatenate([gather_rows(extended, senders), gather_rows(latent, receivers), edge_latent.reshape(N_PATCH, EDGE_DEV, D)], 2)
        message = network(inputs.reshape(-1, 3 * D), edge_inner, edge_outer).reshape(N_PATCH, EDGE_DEV, D)
        message = jnp.where(live_slots[:, :, None], message, 0.0)
        summed = jax.vmap(add_rows)(message, receivers).astype(jnp.bfloat16)
        node_inputs = jnp.concatenate([latent, summed], 2).reshape(-1, 2 * D)
        change = network(node_inputs, node_inner, node_outer).reshape(N_PATCH, NODE_DEV, D)
        updated = (latent.astype(jnp.float32) + change).astype(jnp.bfloat16)
        grid_inputs = jnp.concatenate([gather_rows(extend(updated), grid_rows), grid_edge_latent.reshape(N_PATCH, DEC_DEV, D)], 2)
        grid_message = network(grid_inputs.reshape(-1, 2 * D), grid_inner, grid_outer)
        grid_sum = grid_message.reshape(-1, 3, D).sum(1).astype(jnp.bfloat16)
        output = lax.dot_general(out_weight, grid_sum, (((1,), (1,)), ((), ())), preferred_element_type=jnp.float32)
        return prior_state + output - target
    difference = lax.map(member, mesh_latent.reshape(MEMBERS, N_PATCH, NODE_DEV, D))

    def bracket(own_diff):
        return smooth_slope(own_diff) - lax.optimization_barrier(jnp.sum(smooth_slope(own_diff[None] - difference), 0)) / (MEMBERS - 1)
    result = lax.map(bracket, difference)
    return result * channel_weight[None, :, None] * area_weight[None, None, :]
```

```python
import functools

import jax
import jax.numpy as jnp
from jax import lax
from jax.experimental import pallas as pl
from jax.experimental.pallas import tpu as pltpu
from jax.sharding import PartitionSpec as P

epsilon = 1e-05
smooth = 0.25
f32, bf16 = jnp.float32, jnp.bfloat16
MESH = pl.DeviceIdType.MESH

LANES = 128
WIDTH = 512
NODES = 512
EDGES = 1024
DECODER = 1536
HALO = 96
SENT = 2 * HALO
TABLE = 256
POINTS = 512
CHANNELS = 87
PADDED = 96
HALF = 48
MEMBERS = 8
EDGE_TILE = 256
GRID_TILE = 384
NODE_TILE = 256


def dot(a, b):
    return jnp.dot(a, b, preferred_element_type=f32)


def spread(row):
    return jnp.broadcast_to(row, (LANES, LANES)).T


def one_hot(rows, base, blocks):
    lanes = lax.broadcasted_iota(jnp.int32, rows.shape, 1)
    parts = [
        jnp.where(rows == lanes + (base + LANES * b), 1.0, 0.0).astype(bf16)
        for b in range(blocks)
    ]
    return parts[0] if blocks == 1 else jnp.concatenate(parts, 1)


def silu(v):
    half = 0.5 * v
    return (half + half * jnp.tanh(half)).astype(bf16)


def inverse_spread(centred):
    return lax.rsqrt(jnp.mean(centred * centred, -1, keepdims=True) + epsilon)


def centre(weight):
    wide = weight.astype(f32)
    return (wide - jnp.mean(wide, -1, keepdims=True)).astype(bf16)


def slope(v):
    return v * lax.rsqrt(v * v + smooth * smooth)


def kernel(
    lat_h, elat_h, glat_h, ei_h, eo_h, ni_h, no_h, gi_h, go_h, ow_h, prior_h, target_h,
    cw_h, aw_h, sends_h, es_h, er_h, gs_h, count_s,
    out_ref,
    lat, elat, glat, ws, wr, wp, eo, ni, no, gws, gwp, go, ow, prior, target, cw, aw, sends, es, er, gs,
    chosen, halo, chosen_new, halo_new, table, acc, acc_grid, live, message, updated, readout,
    diff, outgoing, incoming, pairs, answers,
    load_sem, send_sem, recv_sem, send_new_sem, recv_new_sem, out_sem, in_sem, back_sem, answer_sem,
):
    member = lax.axis_index("mem")
    band = lax.axis_index("patch")
    bands = lax.axis_size("patch")
    above = lax.rem(band + 1, bands)
    below = lax.rem(band + bands - 1, bands)

    loads = {}

    def load(name, source, target_ref):
        copy = pltpu.make_async_copy(source, target_ref, load_sem.at[len(loads)])
        copy.start()
        loads[name] = copy

    def ready(*names):
        for name in names:
            loads[name].wait()

    load("sends", sends_h.at[0], sends)
    load("lat", lat_h.at[0], lat)
    load("ws", ei_h.at[pl.ds(0, WIDTH)], ws)
    load("wr", ei_h.at[pl.ds(WIDTH, WIDTH)], wr)
    load("es", es_h, es)
    load("er", er_h, er)
    load("we", ei_h.at[pl.ds(2 * WIDTH, WIDTH)], wp.at[pl.ds(0, WIDTH)])
    load("elat", elat_h, elat)
    load("eo", eo_h, eo)
    load("ni", ni_h, ni)
    load("no", no_h, no)
    load("gws", gi_h.at[pl.ds(0, WIDTH)], gws)
    load("gwe", gi_h.at[pl.ds(WIDTH, WIDTH)], gwp.at[pl.ds(0, WIDTH)])
    load("gs", gs_h, gs)
    load("glat", glat_h, glat)
    load("go", go_h, go)
    load("ow", ow_h, ow)
    load("prior", prior_h, prior)
    load("target", target_h, target)
    load("cw", cw_h, cw)
    load("aw", aw_h, aw)

    barrier = pltpu.get_barrier_semaphore()
    for neighbour in (above, below):
        pl.semaphore_signal(barrier, inc=1, device_id=(member, neighbour), device_id_type=MESH)
    for k in range(1, MEMBERS):
        peer = lax.rem(member + k, MEMBERS)
        pl.semaphore_signal(barrier, inc=1, device_id=(peer, band), device_id_type=MESH)

    ready("sends")
    up = spread(jnp.concatenate([sends[0:1, :], jnp.zeros((1, LANES - HALO), jnp.int32)], 1))
    down = spread(jnp.concatenate([sends[1:2, :], jnp.zeros((1, LANES - HALO), jnp.int32)], 1))
    sent_rows = jnp.concatenate([up[:HALO], down[:HALO]], 0)
    halo[SENT:, :] = jnp.zeros((TABLE - SENT, WIDTH), bf16)
    halo_new[SENT:, :] = jnp.zeros((TABLE - SENT, WIDTH), bf16)
    ready("lat")
    chosen[...] = dot(one_hot(sent_rows, 0, NODES // LANES), lat[...]).astype(bf16)

    pl.semaphore_wait(barrier, MEMBERS + 1)

    def exchange(source, into, send, recv):
        copies = []
        for i, neighbour in enumerate((above, below)):
            copy = pltpu.make_async_remote_copy(
                src_ref=source.at[pl.ds(i * HALO, HALO)],
                dst_ref=into.at[pl.ds(i * HALO, HALO)],
                send_sem=send.at[i],
                recv_sem=recv.at[i],
                device_id=(member, neighbour),
                device_id_type=MESH,
            )
            copy.start()
            copies.append(copy)
        return copies

    first = exchange(chosen, halo, send_sem, recv_sem)

    ready("ws", "wr", "es", "er")
    wp[pl.ds(WIDTH, WIDTH), :] = dot(lat[...], ws[...]).astype(bf16)
    wp[pl.ds(2 * WIDTH, WIDTH), :] = dot(lat[...], wr[...]).astype(bf16)
    count = count_s[0]
    slots = (
        lax.broadcasted_iota(jnp.int32, (EDGES // LANES, LANES), 0) * LANES
        + lax.broadcasted_iota(jnp.int32, (EDGES // LANES, LANES), 1)
    )
    live[...] = jnp.where(slots < count, er[...], -1)
    ready("we", "elat")

    def edge_rows(t, indices):
        each = EDGE_TILE // LANES
        return jnp.concatenate(
            [spread(indices[pl.ds(t * each + i, 1), :]) for i in range(each)], 0
        )

    for t in range(EDGES // EDGE_TILE):
        rows = pl.ds(t * EDGE_TILE, EDGE_TILE)
        picks = [
            elat[rows, :],
            one_hot(edge_rows(t, es), 0, NODES // LANES),
            one_hot(edge_rows(t, er), 0, NODES // LANES),
        ]
        acc[rows, :] = dot(jnp.concatenate(picks, 1), wp[...])
    ready("eo")
    eo[...] = centre(eo[...])
    for copy in first:
        copy.wait()

    table[...] = dot(halo[...], ws[...]).astype(bf16)
    for t in range(EDGES // EDGE_TILE):
        rows = pl.ds(t * EDGE_TILE, EDGE_TILE)
        inner = silu(
            acc[rows, :] + dot(one_hot(edge_rows(t, es), NODES, TABLE // LANES), table[...])
        )
        outer = dot(inner, eo[...])
        message[rows, :] = (outer * inverse_spread(outer)).astype(bf16)

    ready("ni", "no")
    no[...] = centre(no[...])

    def node_update(latent, placing):
        summed = dot(placing, message[...]).astype(bf16)
        inner = silu(dot(jnp.concatenate([latent, summed], 1), ni[...]))
        outer = dot(inner, no[...])
        return (latent.astype(f32) + outer * inverse_spread(outer)).astype(bf16)

    def placing(nodes):
        blocks = [
            jnp.where(nodes == live[i : i + 1, :], 1.0, 0.0).astype(bf16)
            for i in range(EDGES // LANES)
        ]
        return jnp.concatenate(blocks, 1)

    chosen_new[...] = node_update(chosen[...], placing(sent_rows))
    second = exchange(chosen_new, halo_new, send_new_sem, recv_new_sem)

    for t in range(NODES // NODE_TILE):
        rows = pl.ds(t * NODE_TILE, NODE_TILE)
        nodes = lax.broadcasted_iota(jnp.int32, (NODE_TILE, LANES), 0) + t * NODE_TILE
        updated[rows, :] = node_update(lat[rows, :], placing(nodes))
    ready("gws", "gwe", "gs", "glat")
    gwp[pl.ds(WIDTH, WIDTH), :] = dot(updated[...], gws[...]).astype(bf16)

    def grid_rows(t):
        each = GRID_TILE // LANES
        return jnp.concatenate([spread(gs[pl.ds(t * each + i, 1), :]) for i in range(each)], 0)

    for t in range(DECODER // GRID_TILE):
        rows = pl.ds(t * GRID_TILE, GRID_TILE)
        picks = [glat[rows, :], one_hot(grid_rows(t), 0, NODES // LANES)]
        acc_grid[rows, :] = dot(jnp.concatenate(picks, 1), gwp[...])
    ready("go", "ow", "prior", "target", "cw", "aw")
    go[...] = centre(go[...])
    for copy in second:
        copy.wait()

    table[...] = dot(halo_new[...], gws[...]).astype(bf16)
    diff[pl.ds(PADDED - 16, 16), :] = jnp.zeros((16, POINTS), f32)
    for t in range(DECODER // GRID_TILE):
        rows = pl.ds(t * GRID_TILE, GRID_TILE)
        inner = silu(
            acc_grid[rows, :] + dot(one_hot(grid_rows(t), NODES, TABLE // LANES), table[...])
        )
        outer = dot(inner, go[...])
        channels = lax.dot_general(
            outer.astype(bf16), ow[...], (((1,), (1,)), ((), ())), preferred_element_type=f32
        )
        readout[rows, 0:CHANNELS] = channels * inverse_spread(outer)
        points = pl.ds(t * LANES, LANES)
        output = (
            readout[pl.ds(t * GRID_TILE, LANES, 3), :]
            + readout[pl.ds(t * GRID_TILE + 1, LANES, 3), :]
            + readout[pl.ds(t * GRID_TILE + 2, LANES, 3), :]
        )
        diff[0:CHANNELS, points] = (
            prior[:, points] + output.T[0:CHANNELS] - target[:, points]
        )
        for half in range(2):
            outgoing[2 * t + half] = diff[pl.ds(half * HALF, HALF), points].astype(bf16)

    sent = []
    for k in range(1, MEMBERS):
        peer = lax.rem(member + k, MEMBERS)
        copy = pltpu.make_async_remote_copy(
            src_ref=outgoing.at[peer],
            dst_ref=incoming.at[k],
            send_sem=out_sem.at[k],
            recv_sem=in_sem.at[k],
            device_id=(peer, band),
            device_id_type=MESH,
        )
        copy.start()
        sent.append(copy)
    incoming[0] = outgoing[member]
    for copy in sent:
        copy.wait()
    values = [incoming[k].astype(f32) for k in range(MEMBERS)]
    sums = [None] * MEMBERS
    for m in range(MEMBERS):
        for n in range(m):
            term = slope(values[m] - values[n])
            sums[m] = term if sums[m] is None else sums[m] + term
            sums[n] = -term if sums[n] is None else sums[n] - term
    for m in range(MEMBERS):
        pairs[m] = sums[m].astype(bf16)
    sent = []
    for k in range(1, MEMBERS):
        owner = lax.rem(member + MEMBERS - k, MEMBERS)
        copy = pltpu.make_async_remote_copy(
            src_ref=pairs.at[k],
            dst_ref=answers.at[member],
            send_sem=back_sem.at[k],
            recv_sem=answer_sem.at[k],
            device_id=(owner, band),
            device_id_type=MESH,
        )
        copy.start()
        sent.append(copy)
    answers[member] = pairs[0]
    gains = spread(
        jnp.concatenate([cw[...], jnp.zeros((1, LANES - CHANNELS), f32)], 1)
    )
    for copy in sent:
        copy.wait()
    for t in range(POINTS // LANES):
        points = pl.ds(t * LANES, LANES)
        pairwise = jnp.concatenate(
            [answers[2 * t].astype(f32), answers[2 * t + 1].astype(f32)], 0
        )
        result = slope(diff[:, points]) - pairwise * (1.0 / (MEMBERS - 1))
        result = result * gains[:PADDED] * aw[t : t + 1, :]
        out_ref[0, :, points] = result[0:CHANNELS]


def per_device(
    mesh_latent, edge_latent, grid_edge_latent, edge_inner, edge_outer, node_inner, node_outer,
    grid_inner, grid_outer, out_weight, prior_state, target, channel_weight, area_weight,
    send_rows, edge_senders, edge_receivers, edge_count, grid_senders,
):
    hbm = pl.BlockSpec(memory_space=pl.ANY)
    dma = pltpu.SemaphoreType.DMA
    vmem = pltpu.VMEM
    square = vmem((WIDTH, WIDTH), bf16)
    scratch = [
        square,
        vmem((EDGES, WIDTH), bf16),
        vmem((DECODER, WIDTH), bf16),
        square,
        square,
        vmem((3 * WIDTH, WIDTH), bf16),
        square,
        vmem((2 * WIDTH, WIDTH), bf16),
        square,
        square,
        vmem((2 * WIDTH, WIDTH), bf16),
        square,
        vmem((CHANNELS, WIDTH), bf16),
        vmem((CHANNELS, POINTS), f32),
        vmem((CHANNELS, POINTS), f32),
        vmem((1, CHANNELS), f32),
        vmem((POINTS // LANES, LANES), f32),
        vmem((2, HALO), jnp.int32),
        vmem((EDGES // LANES, LANES), jnp.int32),
        vmem((EDGES // LANES, LANES), jnp.int32),
        vmem((DECODER // LANES, LANES), jnp.int32),
        vmem((SENT, WIDTH), bf16),
        vmem((TABLE, WIDTH), bf16),
        vmem((SENT, WIDTH), bf16),
        vmem((TABLE, WIDTH), bf16),
        vmem((TABLE, WIDTH), bf16),
        vmem((EDGES, WIDTH), f32),
        vmem((DECODER, WIDTH), f32),
        vmem((EDGES // LANES, LANES), jnp.int32),
        vmem((EDGES, WIDTH), bf16),
        vmem((NODES, WIDTH), bf16),
        vmem((DECODER, LANES), f32),
        vmem((PADDED, POINTS), f32),
        vmem((MEMBERS, HALF, LANES), bf16),
        vmem((MEMBERS, HALF, LANES), bf16),
        vmem((MEMBERS, HALF, LANES), bf16),
        vmem((MEMBERS, HALF, LANES), bf16),
        dma((21,)),
        dma((2,)),
        dma((2,)),
        dma((2,)),
        dma((2,)),
        dma((MEMBERS,)),
        dma((MEMBERS,)),
        dma((MEMBERS,)),
        dma((MEMBERS,)),
    ]
    return pl.pallas_call(
        kernel,
        out_shape=jax.ShapeDtypeStruct((1, CHANNELS, POINTS), f32),
        in_specs=[hbm] * 18 + [pl.BlockSpec(memory_space=pltpu.SMEM)],
        out_specs=pl.BlockSpec(memory_space=pltpu.VMEM),
        scratch_shapes=scratch,
        compiler_params=pltpu.CompilerParams(
            collective_id=0, has_side_effects=True, vmem_limit_bytes=48 * 1024 * 1024
        ),
        cost_estimate=pl.CostEstimate(
            flops=9_000_000_000, bytes_accessed=9_000_000, transcendentals=2_000_000
        ),
        name="ensemble_layers",
    )(
        mesh_latent, edge_latent, grid_edge_latent, edge_inner, edge_outer, node_inner, node_outer,
        grid_inner, grid_outer, out_weight, prior_state, target,
        channel_weight.reshape(1, CHANNELS),
        area_weight.reshape(POINTS // LANES, LANES),
        send_rows,
        edge_senders.reshape(EDGES // LANES, LANES),
        edge_receivers.reshape(EDGES // LANES, LANES),
        grid_senders.reshape(DECODER // LANES, LANES),
        edge_count,
    )


def solution(mesh):
    in_specs = (
        P("mem", "patch", None),
        P("patch", None),
        P("patch", None),
        P(),
        P(),
        P(),
        P(),
        P(),
        P(),
        P(),
        P(None, "patch"),
        P(None, "patch"),
        P(),
        P("patch"),
        P("patch", None, None),
        P("patch"),
        P("patch"),
        P("patch"),
        P("patch"),
    )
    out_specs = P("mem", None, "patch")
    return jax.shard_map(
        per_device, mesh=mesh, in_specs=in_specs, out_specs=out_specs, check_vma=False
    )
```

```python
import functools

import jax
import jax.numpy as jnp
from jax import lax
from jax.experimental import pallas as pl
from jax.experimental.pallas import tpu as pltpu
from jax.sharding import PartitionSpec as P

epsilon = 1e-05
smooth = 0.25
f32, bf16 = jnp.float32, jnp.bfloat16
MESH = pl.DeviceIdType.MESH

LANES = 128
WIDTH = 512
NODES = 512
EDGES = 1024
DECODER = 1536
HALO = 96
SENT = 2 * HALO
TABLE = 256
POINTS = 512
CHANNELS = 87
PADDED = 96
MEMBERS = 8
PEERS = 3
CHUNKS = 2
CHUNK = POINTS // CHUNKS
EDGE_TILE = 256
GRID_TILE = 384
NODE_TILE = 256


def dot(a, b):
    return jnp.dot(a, b, preferred_element_type=f32)


def spread(row):
    return jnp.broadcast_to(row, (LANES, LANES)).T


def one_hot(rows, base, blocks):
    lanes = lax.broadcasted_iota(jnp.int32, rows.shape, 1)
    parts = [
        jnp.where(rows == lanes + (base + LANES * b), 1.0, 0.0).astype(bf16)
        for b in range(blocks)
    ]
    return parts[0] if blocks == 1 else jnp.concatenate(parts, 1)


def silu(v):
    half = 0.5 * v
    return (half + half * jnp.tanh(half)).astype(bf16)


def inverse_spread(centred):
    return lax.rsqrt(jnp.mean(centred * centred, -1, keepdims=True) + epsilon)


def centre(weight):
    wide = weight.astype(f32)
    return (wide - jnp.mean(wide, -1, keepdims=True)).astype(bf16)


def slope(v):
    return v * lax.rsqrt(v * v + smooth * smooth)


def kernel(
    lat_h, elat_h, glat_h, ei_h, eo_h, ni_h, no_h, gi_h, go_h, ow_h, prior_h, target_h,
    cw_h, aw_h, sends_h, es_h, er_h, gs_h, count_h,
    out_ref,
    lat, elat, glat, ws, wr, wp, eo, ni, no, gws, gwp, go, ow, prior, target, cw, aw, sends, es, er, gs, count,
    chosen, halo, chosen_new, halo_new, table, acc, acc_grid, live, message, updated, readout,
    diff, outgoing, incoming, beside, pairwise, partial, partial_in,
    load_sem, send_sem, recv_sem, send_new_sem, recv_new_sem, peer_sem, peer_in_sem, beside_sem, beside_in_sem,
    partial_sem, partial_in_sem,
):
    member = lax.axis_index("mem")
    band = lax.axis_index("patch")
    bands = lax.axis_size("patch")
    above = band + 1
    below = band - 1
    has_above = band < bands - 1
    has_below = band > 0
    sibling = member + 1 - 2 * lax.rem(member, 2)
    peers = [lax.rem(member + 2 * k, MEMBERS) for k in range(1, PEERS + 1)]

    barrier = pltpu.get_barrier_semaphore()

    def greet(other, row):
        pl.semaphore_signal(barrier, inc=1, device_id=(other, row), device_id_type=MESH)

    @pl.when(has_above)
    def _():
        greet(member, above)

    @pl.when(has_below)
    def _():
        greet(member, below)

    for other in peers + [sibling]:
        greet(other, band)

    loads = {}

    def load(name, source, target_ref):
        copy = pltpu.make_async_copy(source, target_ref, load_sem.at[len(loads)])
        copy.start()
        loads[name] = copy

    def ready(*names):
        for name in names:
            loads[name].wait()

    load("sends", sends_h.at[0], sends)
    load("lat", lat_h.at[0], lat)
    load("ws", ei_h.at[pl.ds(0, WIDTH)], ws)
    load("wr", ei_h.at[pl.ds(WIDTH, WIDTH)], wr)
    load("es", es_h, es)
    load("er", er_h, er)
    load("count", count_h, count)
    load("we", ei_h.at[pl.ds(2 * WIDTH, WIDTH)], wp.at[pl.ds(0, WIDTH)])
    load("elat", elat_h, elat)
    ready("sends")
    up = spread(jnp.concatenate([sends[0:1, :], jnp.zeros((1, LANES - HALO), jnp.int32)], 1))
    down = spread(jnp.concatenate([sends[1:2, :], jnp.zeros((1, LANES - HALO), jnp.int32)], 1))
    sent_rows = jnp.concatenate([up[:HALO], down[:HALO]], 0)
    for rows in (halo, halo_new):
        rows[SENT:, :] = jnp.zeros((TABLE - SENT, WIDTH), bf16)

        @pl.when(jnp.logical_not(has_below))
        def _():
            rows[:HALO, :] = jnp.zeros((HALO, WIDTH), bf16)

        @pl.when(jnp.logical_not(has_above))
        def _():
            rows[HALO:SENT, :] = jnp.zeros((HALO, WIDTH), bf16)

    ready("lat")
    chosen[...] = dot(one_hot(sent_rows, 0, NODES // LANES), lat[...]).astype(bf16)

    pl.semaphore_wait(
        barrier, PEERS + 1 + has_above.astype(jnp.int32) + has_below.astype(jnp.int32)
    )

    def remote(source, into, send, recv, other, row):
        return pltpu.make_async_remote_copy(
            src_ref=source,
            dst_ref=into,
            send_sem=send,
            recv_sem=recv,
            device_id=(other, row),
            device_id_type=MESH,
        )

    def exchange(source, into, send, recv):
        copies = []
        for i, (there, neighbour) in enumerate(((has_above, above), (has_below, below))):
            part = pl.ds(i * HALO, HALO)
            copy = remote(source.at[part], into.at[part], send.at[i], recv.at[i], member, neighbour)
            copies.append(copy)

            @pl.when(there)
            def _():
                copy.start()

        return copies

    def arrived(copies):
        for copy, there in zip(copies, (has_below, has_above)):

            @pl.when(there)
            def _():
                copy.wait_recv()

    def left(copies):
        for copy, there in zip(copies, (has_above, has_below)):

            @pl.when(there)
            def _():
                copy.wait_send()

    first = exchange(chosen, halo, send_sem, recv_sem)

    load("eo", eo_h, eo)
    load("ni", ni_h, ni)
    load("no", no_h, no)
    load("gws", gi_h.at[pl.ds(0, WIDTH)], gws)
    load("gwe", gi_h.at[pl.ds(WIDTH, WIDTH)], gwp.at[pl.ds(0, WIDTH)])
    load("gs", gs_h, gs)
    load("glat", glat_h, glat)
    load("go", go_h, go)
    load("ow", ow_h, ow)
    load("prior", prior_h, prior)
    load("target", target_h, target)
    load("cw", cw_h, cw)
    load("aw", aw_h, aw)
    ready("ws", "wr", "es", "er", "count")
    wp[pl.ds(WIDTH, WIDTH), :] = dot(lat[...], ws[...]).astype(bf16)
    wp[pl.ds(2 * WIDTH, WIDTH), :] = dot(lat[...], wr[...]).astype(bf16)
    slots = (
        lax.broadcasted_iota(jnp.int32, (EDGES // LANES, LANES), 0) * LANES
        + lax.broadcasted_iota(jnp.int32, (EDGES // LANES, LANES), 1)
    )
    live[...] = jnp.where(slots < count[...], er[...], -1)
    ready("we", "elat")

    def edge_rows(t, indices):
        each = EDGE_TILE // LANES
        return jnp.concatenate(
            [spread(indices[pl.ds(t * each + i, 1), :]) for i in range(each)], 0
        )

    for t in range(EDGES // EDGE_TILE):
        rows = pl.ds(t * EDGE_TILE, EDGE_TILE)
        picks = [
            elat[rows, :],
            one_hot(edge_rows(t, es), 0, NODES // LANES),
            one_hot(edge_rows(t, er), 0, NODES // LANES),
        ]
        acc[rows, :] = dot(jnp.concatenate(picks, 1), wp[...])
    ready("eo")
    eo[...] = centre(eo[...])
    arrived(first)

    table[...] = dot(halo[...], ws[...]).astype(bf16)
    for t in range(EDGES // EDGE_TILE):
        rows = pl.ds(t * EDGE_TILE, EDGE_TILE)
        inner = silu(
            acc[rows, :] + dot(one_hot(edge_rows(t, es), NODES, TABLE // LANES), table[...])
        )
        outer = dot(inner, eo[...])
        message[rows, :] = (outer * inverse_spread(outer)).astype(bf16)

    ready("ni", "no")
    no[...] = centre(no[...])

    def node_update(latent, placing):
        summed = dot(placing, message[...]).astype(bf16)
        inner = silu(dot(jnp.concatenate([latent, summed], 1), ni[...]))
        outer = dot(inner, no[...])
        return (latent.astype(f32) + outer * inverse_spread(outer)).astype(bf16)

    def placing(nodes):
        blocks = [
            jnp.where(nodes == live[i : i + 1, :], 1.0, 0.0).astype(bf16)
            for i in range(EDGES // LANES)
        ]
        return jnp.concatenate(blocks, 1)

    chosen_new[...] = node_update(chosen[...], placing(sent_rows))
    second = exchange(chosen_new, halo_new, send_new_sem, recv_new_sem)

    for t in range(NODES // NODE_TILE):
        rows = pl.ds(t * NODE_TILE, NODE_TILE)
        nodes = lax.broadcasted_iota(jnp.int32, (NODE_TILE, LANES), 0) + t * NODE_TILE
        updated[rows, :] = node_update(lat[rows, :], placing(nodes))
    ready("gws", "gwe", "gs", "glat")
    gwp[pl.ds(WIDTH, WIDTH), :] = dot(updated[...], gws[...]).astype(bf16)

    def grid_rows(t):
        each = GRID_TILE // LANES
        return jnp.concatenate([spread(gs[pl.ds(t * each + i, 1), :]) for i in range(each)], 0)

    for t in range(DECODER // GRID_TILE):
        rows = pl.ds(t * GRID_TILE, GRID_TILE)
        picks = [glat[rows, :], one_hot(grid_rows(t), 0, NODES // LANES)]
        acc_grid[rows, :] = dot(jnp.concatenate(picks, 1), gwp[...])
    ready("go", "ow", "prior", "target", "cw", "aw")
    go[...] = centre(go[...])
    arrived(second)

    table[...] = dot(halo_new[...], gws[...]).astype(bf16)
    diff[pl.ds(PADDED - 16, 16), :] = jnp.zeros((16, POINTS), f32)
    to_peers, to_sibling, to_partial = [], [], []
    for t in range(DECODER // GRID_TILE):
        rows = pl.ds(t * GRID_TILE, GRID_TILE)
        inner = silu(
            acc_grid[rows, :] + dot(one_hot(grid_rows(t), NODES, TABLE // LANES), table[...])
        )
        outer = dot(inner, go[...])
        channels = lax.dot_general(
            outer.astype(bf16), ow[...], (((1,), (1,)), ((), ())), preferred_element_type=f32
        )
        readout[rows, 0:CHANNELS] = channels * inverse_spread(outer)
        points = pl.ds(t * LANES, LANES)
        output = (
            readout[pl.ds(t * GRID_TILE, LANES, 3), :]
            + readout[pl.ds(t * GRID_TILE + 1, LANES, 3), :]
            + readout[pl.ds(t * GRID_TILE + 2, LANES, 3), :]
        )
        diff[0:CHANNELS, points] = (
            prior[:, points] + output.T[0:CHANNELS] - target[:, points]
        )
        chunk, part = divmod(t * LANES, CHUNK)
        outgoing[chunk, :, pl.ds(part, LANES)] = diff[:, points].astype(bf16)
        if part + LANES == CHUNK:
            to_peers.append([
                remote(
                    outgoing.at[chunk], incoming.at[chunk, k], peer_sem.at[chunk, k],
                    peer_in_sem.at[chunk, k], peers[k], band,
                )
                for k in (1, 0, 2)
            ])
            to_sibling.append(
                remote(
                    outgoing.at[chunk], beside.at[chunk], beside_sem.at[chunk],
                    beside_in_sem.at[chunk], sibling, band,
                )
            )
            for copy in to_peers[-1] + to_sibling[-1:]:
                copy.start()

    gains = spread(
        jnp.concatenate([cw[...], jnp.zeros((1, LANES - CHANNELS), f32)], 1)
    )
    blocks = [pl.ds(part, LANES) for part in range(0, CHUNK, LANES)]
    for chunk in range(CHUNKS):
        to_sibling[chunk].wait_recv()
        for copy in to_peers[chunk]:
            copy.wait_recv()
        for block in blocks:
            near = beside[chunk, :, block].astype(f32)
            total = None
            for k in range(PEERS):
                term = slope(near - incoming[chunk, k, :, block].astype(f32))
                total = term if total is None else total + term
            partial[chunk, :, block] = total.astype(bf16)
        copy = remote(
            partial.at[chunk], partial_in.at[chunk], partial_sem.at[chunk],
            partial_in_sem.at[chunk], sibling, band,
        )
        copy.start()
        to_partial.append(copy)
        for block in blocks:
            points = pl.ds(chunk * CHUNK + block.start, LANES)
            own = diff[:, points]
            total = slope(own - beside[chunk, :, block].astype(f32))
            for k in range(PEERS):
                total = total + slope(own - incoming[chunk, k, :, block].astype(f32))
            pairwise[:, points] = slope(own) - total * (1.0 / (MEMBERS - 1))
    for chunk in range(CHUNKS):
        to_partial[chunk].wait_recv()
        for block in blocks:
            points = pl.ds(chunk * CHUNK + block.start, LANES)
            t = (chunk * CHUNK + block.start) // LANES
            result = pairwise[:, points] - partial_in[chunk, :, block].astype(f32) * (
                1.0 / (MEMBERS - 1)
            )
            result = result * gains[:PADDED] * aw[t : t + 1, :]
            out_ref[0, :, points] = result[0:CHANNELS]
    left(first)
    left(second)
    for chunk in range(CHUNKS):
        for copy in to_peers[chunk] + [to_sibling[chunk], to_partial[chunk]]:
            copy.wait_send()


def per_device(
    mesh_latent, edge_latent, grid_edge_latent, edge_inner, edge_outer, node_inner, node_outer,
    grid_inner, grid_outer, out_weight, prior_state, target, channel_weight, area_weight,
    send_rows, edge_senders, edge_receivers, edge_count, grid_senders,
):
    hbm = pl.BlockSpec(memory_space=pltpu.HBM)
    dma = pltpu.SemaphoreType.DMA
    vmem = pltpu.VMEM
    square = vmem((WIDTH, WIDTH), bf16)
    scratch = [
        square,
        vmem((EDGES, WIDTH), bf16),
        vmem((DECODER, WIDTH), bf16),
        square,
        square,
        vmem((3 * WIDTH, WIDTH), bf16),
        square,
        vmem((2 * WIDTH, WIDTH), bf16),
        square,
        square,
        vmem((2 * WIDTH, WIDTH), bf16),
        square,
        vmem((CHANNELS, WIDTH), bf16),
        vmem((CHANNELS, POINTS), f32),
        vmem((CHANNELS, POINTS), f32),
        vmem((1, CHANNELS), f32),
        vmem((POINTS // LANES, LANES), f32),
        vmem((2, HALO), jnp.int32),
        vmem((EDGES // LANES, LANES), jnp.int32),
        vmem((EDGES // LANES, LANES), jnp.int32),
        vmem((DECODER // LANES, LANES), jnp.int32),
        vmem((1, 1), jnp.int32),
        vmem((SENT, WIDTH), bf16),
        vmem((TABLE, WIDTH), bf16),
        vmem((SENT, WIDTH), bf16),
        vmem((TABLE, WIDTH), bf16),
        vmem((TABLE, WIDTH), bf16),
        vmem((EDGES, WIDTH), f32),
        vmem((DECODER, WIDTH), f32),
        vmem((EDGES // LANES, LANES), jnp.int32),
        vmem((EDGES, WIDTH), bf16),
        vmem((NODES, WIDTH), bf16),
        vmem((DECODER, LANES), f32),
        vmem((PADDED, POINTS), f32),
        vmem((CHUNKS, PADDED, CHUNK), bf16),
        vmem((CHUNKS, PEERS, PADDED, CHUNK), bf16),
        vmem((CHUNKS, PADDED, CHUNK), bf16),
        vmem((PADDED, POINTS), f32),
        vmem((CHUNKS, PADDED, CHUNK), bf16),
        vmem((CHUNKS, PADDED, CHUNK), bf16),
        dma((22,)),
        dma((2,)),
        dma((2,)),
        dma((2,)),
        dma((2,)),
        dma((CHUNKS, PEERS)),
        dma((CHUNKS, PEERS)),
        dma((CHUNKS,)),
        dma((CHUNKS,)),
        dma((CHUNKS,)),
        dma((CHUNKS,)),
    ]
    return pl.pallas_call(
        kernel,
        out_shape=jax.ShapeDtypeStruct((1, CHANNELS, POINTS), f32),
        in_specs=[hbm] * 19,
        out_specs=pl.BlockSpec(memory_space=pltpu.VMEM),
        scratch_shapes=scratch,
        compiler_params=pltpu.CompilerParams(
            collective_id=0, has_side_effects=True, vmem_limit_bytes=60 * 1024 * 1024
        ),
        cost_estimate=pl.CostEstimate(
            flops=9_000_000_000, bytes_accessed=9_000_000, transcendentals=2_000_000
        ),
        name="ensemble_layers",
    )(
        mesh_latent, edge_latent, grid_edge_latent, edge_inner, edge_outer, node_inner, node_outer,
        grid_inner, grid_outer, out_weight, prior_state, target,
        channel_weight.reshape(1, CHANNELS),
        area_weight.reshape(POINTS // LANES, LANES),
        send_rows,
        edge_senders.reshape(EDGES // LANES, LANES),
        edge_receivers.reshape(EDGES // LANES, LANES),
        grid_senders.reshape(DECODER // LANES, LANES),
        edge_count.reshape(1, 1),
    )


def solution(mesh):
    in_specs = (
        P("mem", "patch", None),
        P("patch", None),
        P("patch", None),
        P(),
        P(),
        P(),
        P(),
        P(),
        P(),
        P(),
        P(None, "patch"),
        P(None, "patch"),
        P(),
        P("patch"),
        P("patch", None, None),
        P("patch"),
        P("patch"),
        P("patch"),
        P("patch"),
    )
    out_specs = P("mem", None, "patch")
    return jax.shard_map(
        per_device, mesh=mesh, in_specs=in_specs, out_specs=out_specs, check_vma=False
    )
```

```python
import functools

import jax
import jax.numpy as jnp
from jax import lax
from jax.experimental import pallas as pl
from jax.experimental.pallas import tpu as pltpu
from jax.sharding import PartitionSpec as P

epsilon = 1e-05
smooth = 0.25
f32, bf16 = jnp.float32, jnp.bfloat16
MESH = pl.DeviceIdType.MESH

LANES = 128
WIDTH = 512
NODES = 512
EDGES = 1024
DECODER = 1536
HALO = 96
SENT = 2 * HALO
TABLE = 256
POINTS = 512
CHANNELS = 87
PADDED = 96
MEMBERS = 8
PEERS = 3
CHUNKS = 2
CHUNK = POINTS // CHUNKS
EDGE_TILE = 512
GRID_TILE = 384
NODE_TILE = 256


def dot(a, b):
    return jnp.dot(a, b, preferred_element_type=f32)


def spread(row):
    return jnp.broadcast_to(row, (LANES, LANES)).T


def one_hot(rows, base, blocks):
    lanes = lax.broadcasted_iota(jnp.int32, rows.shape, 1)
    rows = rows.astype(jnp.int16)
    parts = [
        jnp.where(rows == (lanes + (base + LANES * b)).astype(jnp.int16), jnp.ones((), bf16), jnp.zeros((), bf16))
        for b in range(blocks)
    ]
    return parts[0] if blocks == 1 else jnp.concatenate(parts, 1)


def silu(v):
    half = 0.5 * v
    return (half + half * jnp.tanh(half)).astype(bf16)


def inverse_spread(centred):
    return lax.rsqrt(jnp.mean(centred * centred, -1, keepdims=True) + epsilon)


def centre(weight):
    wide = weight.astype(f32)
    return (wide - jnp.mean(wide, -1, keepdims=True)).astype(bf16)


def slope(v):
    return v * lax.rsqrt(v * v + smooth * smooth)


def kernel(
    lat_h, elat_h, glat_h, ei_h, eo_h, ni_h, no_h, gi_h, go_h, ow_h, prior_h, target_h,
    cw_h, aw_h, sends_h, es_h, er_h, gs_h, count_h,
    out_ref,
    lat, elat, glat, ws, wr, wp, eo, ni, no, gws, gwp, go, ow, prior, target, cw, aw, sends, es, er, gs, count,
    chosen, halo, chosen_new, halo_new, table, from_halo, into_sent, grid_from_halo, acc, acc_grid, live, message, updated, readout,
    diff, outgoing, incoming, beside, pairwise, partial, partial_in,
    load_sem, send_sem, recv_sem, send_new_sem, recv_new_sem, peer_sem, peer_in_sem, beside_sem, beside_in_sem,
    partial_sem, partial_in_sem,
):
    member = lax.axis_index("mem")
    band = lax.axis_index("patch")
    bands = lax.axis_size("patch")
    above = band + 1
    below = band - 1
    has_above = band < bands - 1
    has_below = band > 0
    sibling = member + 1 - 2 * lax.rem(member, 2)
    peers = [lax.rem(member + 2 * k, MEMBERS) for k in range(1, PEERS + 1)]

    barrier = pltpu.get_barrier_semaphore()

    def greet(other, row):
        pl.semaphore_signal(barrier, inc=1, device_id=(other, row), device_id_type=MESH)

    @pl.when(has_above)
    def _():
        greet(member, above)

    @pl.when(has_below)
    def _():
        greet(member, below)

    for other in peers + [sibling]:
        greet(other, band)

    loads = {}

    def load(name, source, target_ref):
        copy = pltpu.make_async_copy(source, target_ref, load_sem.at[len(loads)])
        copy.start()
        loads[name] = copy

    def ready(*names):
        for name in names:
            loads[name].wait()

    load("sends", sends_h.at[0], sends)
    load("lat", lat_h.at[0], lat)
    load("ws", ei_h.at[pl.ds(0, WIDTH)], ws)
    load("wr", ei_h.at[pl.ds(WIDTH, WIDTH)], wr)
    load("es", es_h, es)
    load("er", er_h, er)
    load("count", count_h, count)
    load("we", ei_h.at[pl.ds(2 * WIDTH, WIDTH)], wp.at[pl.ds(0, WIDTH)])
    load("elat", elat_h, elat)
    ready("sends")
    up = spread(jnp.concatenate([sends[0:1, :], jnp.zeros((1, LANES - HALO), jnp.int32)], 1))
    down = spread(jnp.concatenate([sends[1:2, :], jnp.zeros((1, LANES - HALO), jnp.int32)], 1))
    sent_rows = jnp.concatenate([up[:HALO], down[:HALO]], 0)
    for rows in (halo, halo_new):
        rows[SENT:, :] = jnp.zeros((TABLE - SENT, WIDTH), bf16)

        @pl.when(jnp.logical_not(has_below))
        def _():
            rows[:HALO, :] = jnp.zeros((HALO, WIDTH), bf16)

        @pl.when(jnp.logical_not(has_above))
        def _():
            rows[HALO:SENT, :] = jnp.zeros((HALO, WIDTH), bf16)

    ready("lat")
    chosen[...] = dot(one_hot(sent_rows, 0, NODES // LANES), lat[...]).astype(bf16)

    pl.semaphore_wait(
        barrier, PEERS + 1 + has_above.astype(jnp.int32) + has_below.astype(jnp.int32)
    )

    def remote(source, into, send, recv, other, row):
        return pltpu.make_async_remote_copy(
            src_ref=source,
            dst_ref=into,
            send_sem=send,
            recv_sem=recv,
            device_id=(other, row),
            device_id_type=MESH,
        )

    def exchange(source, into, send, recv):
        copies = []
        for i, (there, neighbour) in enumerate(((has_above, above), (has_below, below))):
            part = pl.ds(i * HALO, HALO)
            copy = remote(source.at[part], into.at[part], send.at[i], recv.at[i], member, neighbour)
            copies.append(copy)

            @pl.when(there)
            def _():
                copy.start()

        return copies

    def arrived(copies):
        for copy, there in zip(copies, (has_below, has_above)):

            @pl.when(there)
            def _():
                copy.wait_recv()

    def left(copies):
        for copy, there in zip(copies, (has_above, has_below)):

            @pl.when(there)
            def _():
                copy.wait_send()

    first = exchange(chosen, halo, send_sem, recv_sem)

    load("eo", eo_h, eo)
    load("ni", ni_h, ni)
    load("no", no_h, no)
    load("gws", gi_h.at[pl.ds(0, WIDTH)], gws)
    load("gwe", gi_h.at[pl.ds(WIDTH, WIDTH)], gwp.at[pl.ds(0, WIDTH)])
    load("gs", gs_h, gs)
    load("glat", glat_h, glat)
    load("go", go_h, go)
    load("ow", ow_h, ow)
    load("prior", prior_h, prior)
    load("target", target_h, target)
    load("cw", cw_h, cw)
    load("aw", aw_h, aw)
    ready("ws", "wr", "es", "er", "count")
    wp[pl.ds(WIDTH, WIDTH), :] = dot(lat[...], ws[...]).astype(bf16)
    wp[pl.ds(2 * WIDTH, WIDTH), :] = dot(lat[...], wr[...]).astype(bf16)
    slots = (
        lax.broadcasted_iota(jnp.int32, (EDGES // LANES, LANES), 0) * LANES
        + lax.broadcasted_iota(jnp.int32, (EDGES // LANES, LANES), 1)
    )
    live[...] = jnp.where(slots < count[...], er[...], -1)
    ready("we", "elat")

    def edge_rows(t, indices):
        each = EDGE_TILE // LANES
        return jnp.concatenate(
            [spread(indices[pl.ds(t * each + i, 1), :]) for i in range(each)], 0
        )

    for t in range(EDGES // EDGE_TILE):
        rows = pl.ds(t * EDGE_TILE, EDGE_TILE)
        senders = edge_rows(t, es)
        from_halo[rows, :] = one_hot(senders, NODES, TABLE // LANES)
        picks = [
            elat[rows, :],
            one_hot(senders, 0, NODES // LANES),
            one_hot(edge_rows(t, er), 0, NODES // LANES),
        ]
        acc[rows, :] = dot(jnp.concatenate(picks, 1), wp[...])
    ready("eo")
    eo[...] = centre(eo[...])
    ready("ni", "no")
    no[...] = centre(no[...])

    def placing(nodes):
        blocks = [
            jnp.where(nodes == live[i : i + 1, :], 1.0, 0.0).astype(bf16)
            for i in range(EDGES // LANES)
        ]
        return jnp.concatenate(blocks, 1)

    into_sent[...] = placing(sent_rows)
    arrived(first)

    table[...] = dot(halo[...], ws[...]).astype(bf16)
    for t in range(EDGES // EDGE_TILE):
        rows = pl.ds(t * EDGE_TILE, EDGE_TILE)
        inner = silu(
            acc[rows, :] + dot(from_halo[rows, :], table[...])
        )
        outer = dot(inner, eo[...])
        message[rows, :] = (outer * inverse_spread(outer)).astype(bf16)


    def node_update(latent, placing):
        summed = dot(placing, message[...]).astype(bf16)
        inner = silu(dot(jnp.concatenate([latent, summed], 1), ni[...]))
        outer = dot(inner, no[...])
        return (latent.astype(f32) + outer * inverse_spread(outer)).astype(bf16)

    chosen_new[...] = node_update(chosen[...], into_sent[...])
    second = exchange(chosen_new, halo_new, send_new_sem, recv_new_sem)

    for t in range(NODES // NODE_TILE):
        rows = pl.ds(t * NODE_TILE, NODE_TILE)
        nodes = lax.broadcasted_iota(jnp.int32, (NODE_TILE, LANES), 0) + t * NODE_TILE
        updated[rows, :] = node_update(lat[rows, :], placing(nodes))
    ready("gws", "gwe", "gs", "glat")
    gwp[pl.ds(WIDTH, WIDTH), :] = dot(updated[...], gws[...]).astype(bf16)

    def grid_rows(t):
        each = GRID_TILE // LANES
        return jnp.concatenate([spread(gs[pl.ds(t * each + i, 1), :]) for i in range(each)], 0)

    for t in range(DECODER // GRID_TILE):
        rows = pl.ds(t * GRID_TILE, GRID_TILE)
        senders = grid_rows(t)
        grid_from_halo[rows, :] = one_hot(senders, NODES, TABLE // LANES)
        picks = [glat[rows, :], one_hot(senders, 0, NODES // LANES)]
        acc_grid[rows, :] = dot(jnp.concatenate(picks, 1), gwp[...])
    ready("go", "ow", "prior", "target", "cw", "aw")
    go[...] = centre(go[...])
    arrived(second)

    table[...] = dot(halo_new[...], gws[...]).astype(bf16)
    diff[pl.ds(PADDED - 16, 16), :] = jnp.zeros((16, POINTS), f32)
    to_peers, to_sibling, to_partial = [], [], []
    for t in range(DECODER // GRID_TILE):
        rows = pl.ds(t * GRID_TILE, GRID_TILE)
        inner = silu(
            acc_grid[rows, :] + dot(grid_from_halo[rows, :], table[...])
        )
        outer = dot(inner, go[...])
        channels = lax.dot_general(
            outer.astype(bf16), ow[...], (((1,), (1,)), ((), ())), preferred_element_type=f32
        )
        readout[rows, 0:CHANNELS] = channels * inverse_spread(outer)
        points = pl.ds(t * LANES, LANES)
        output = (
            readout[pl.ds(t * GRID_TILE, LANES, 3), :]
            + readout[pl.ds(t * GRID_TILE + 1, LANES, 3), :]
            + readout[pl.ds(t * GRID_TILE + 2, LANES, 3), :]
        )
        diff[0:CHANNELS, points] = (
            prior[:, points] + output.T[0:CHANNELS] - target[:, points]
        )
        chunk, part = divmod(t * LANES, CHUNK)
        outgoing[chunk, :, pl.ds(part, LANES)] = diff[:, points].astype(bf16)
        if part + LANES == CHUNK:
            to_peers.append([
                remote(
                    outgoing.at[chunk], incoming.at[chunk, k], peer_sem.at[chunk, k],
                    peer_in_sem.at[chunk, k], peers[k], band,
                )
                for k in (1, 0, 2)
            ])
            to_sibling.append(
                remote(
                    outgoing.at[chunk], beside.at[chunk], beside_sem.at[chunk],
                    beside_in_sem.at[chunk], sibling, band,
                )
            )
            for copy in to_peers[-1] + to_sibling[-1:]:
                copy.start()

    gains = spread(
        jnp.concatenate([cw[...], jnp.zeros((1, LANES - CHANNELS), f32)], 1)
    )
    blocks = [pl.ds(part, LANES) for part in range(0, CHUNK, LANES)]
    for chunk in range(CHUNKS):
        to_sibling[chunk].wait_recv()
        for copy in to_peers[chunk]:
            copy.wait_recv()
        for block in blocks:
            near = beside[chunk, :, block].astype(f32)
            total = None
            for k in range(PEERS):
                term = slope(near - incoming[chunk, k, :, block].astype(f32))
                total = term if total is None else total + term
            partial[chunk, :, block] = total.astype(bf16)
        copy = remote(
            partial.at[chunk], partial_in.at[chunk], partial_sem.at[chunk],
            partial_in_sem.at[chunk], sibling, band,
        )
        copy.start()
        to_partial.append(copy)
        for block in blocks:
            points = pl.ds(chunk * CHUNK + block.start, LANES)
            own = diff[:, points]
            total = slope(own - beside[chunk, :, block].astype(f32))
            for k in range(PEERS):
                total = total + slope(own - incoming[chunk, k, :, block].astype(f32))
            pairwise[:, points] = slope(own) - total * (1.0 / (MEMBERS - 1))
    for chunk in range(CHUNKS):
        to_partial[chunk].wait_recv()
        for block in blocks:
            points = pl.ds(chunk * CHUNK + block.start, LANES)
            t = (chunk * CHUNK + block.start) // LANES
            result = pairwise[:, points] - partial_in[chunk, :, block].astype(f32) * (
                1.0 / (MEMBERS - 1)
            )
            result = result * gains[:PADDED] * aw[t : t + 1, :]
            out_ref[0, :, points] = result[0:CHANNELS]
    left(first)
    left(second)
    for chunk in range(CHUNKS):
        for copy in to_peers[chunk] + [to_sibling[chunk], to_partial[chunk]]:
            copy.wait_send()


def per_device(
    mesh_latent, edge_latent, grid_edge_latent, edge_inner, edge_outer, node_inner, node_outer,
    grid_inner, grid_outer, out_weight, prior_state, target, channel_weight, area_weight,
    send_rows, edge_senders, edge_receivers, edge_count, grid_senders,
):
    hbm = pl.BlockSpec(memory_space=pltpu.HBM)
    dma = pltpu.SemaphoreType.DMA
    vmem = pltpu.VMEM
    square = vmem((WIDTH, WIDTH), bf16)
    scratch = [
        square,
        vmem((EDGES, WIDTH), bf16),
        vmem((DECODER, WIDTH), bf16),
        square,
        square,
        vmem((3 * WIDTH, WIDTH), bf16),
        square,
        vmem((2 * WIDTH, WIDTH), bf16),
        square,
        square,
        vmem((2 * WIDTH, WIDTH), bf16),
        square,
        vmem((CHANNELS, WIDTH), bf16),
        vmem((CHANNELS, POINTS), f32),
        vmem((CHANNELS, POINTS), f32),
        vmem((1, CHANNELS), f32),
        vmem((POINTS // LANES, LANES), f32),
        vmem((2, HALO), jnp.int32),
        vmem((EDGES // LANES, LANES), jnp.int32),
        vmem((EDGES // LANES, LANES), jnp.int32),
        vmem((DECODER // LANES, LANES), jnp.int32),
        vmem((1, 1), jnp.int32),
        vmem((SENT, WIDTH), bf16),
        vmem((TABLE, WIDTH), bf16),
        vmem((SENT, WIDTH), bf16),
        vmem((TABLE, WIDTH), bf16),
        vmem((TABLE, WIDTH), bf16),
        vmem((EDGES, TABLE), bf16),
        vmem((SENT, EDGES), bf16),
        vmem((DECODER, TABLE), bf16),
        vmem((EDGES, WIDTH), f32),
        vmem((DECODER, WIDTH), f32),
        vmem((EDGES // LANES, LANES), jnp.int32),
        vmem((EDGES, WIDTH), bf16),
        vmem((NODES, WIDTH), bf16),
        vmem((DECODER, LANES), f32),
        vmem((PADDED, POINTS), f32),
        vmem((CHUNKS, PADDED, CHUNK), bf16),
        vmem((CHUNKS, PEERS, PADDED, CHUNK), bf16),
        vmem((CHUNKS, PADDED, CHUNK), bf16),
        vmem((PADDED, POINTS), f32),
        vmem((CHUNKS, PADDED, CHUNK), bf16),
        vmem((CHUNKS, PADDED, CHUNK), bf16),
        dma((22,)),
        dma((2,)),
        dma((2,)),
        dma((2,)),
        dma((2,)),
        dma((CHUNKS, PEERS)),
        dma((CHUNKS, PEERS)),
        dma((CHUNKS,)),
        dma((CHUNKS,)),
        dma((CHUNKS,)),
        dma((CHUNKS,)),
    ]
    return pl.pallas_call(
        kernel,
        out_shape=pltpu.VMEM((1, CHANNELS, POINTS), f32),
        in_specs=[hbm] * 19,
        out_specs=pl.BlockSpec(memory_space=pltpu.VMEM),
        scratch_shapes=scratch,
        compiler_params=pltpu.CompilerParams(
            collective_id=0, has_side_effects=True, vmem_limit_bytes=60 * 1024 * 1024
        ),
        cost_estimate=pl.CostEstimate(
            flops=9_000_000_000, bytes_accessed=9_000_000, transcendentals=2_000_000
        ),
        name="ensemble_layers",
    )(
        mesh_latent, edge_latent, grid_edge_latent, edge_inner, edge_outer, node_inner, node_outer,
        grid_inner, grid_outer, out_weight, prior_state, target,
        channel_weight.reshape(1, CHANNELS),
        area_weight.reshape(POINTS // LANES, LANES),
        send_rows,
        edge_senders.reshape(EDGES // LANES, LANES),
        edge_receivers.reshape(EDGES // LANES, LANES),
        grid_senders.reshape(DECODER // LANES, LANES),
        edge_count.reshape(1, 1),
    )


def solution(mesh):
    in_specs = (
        P("mem", "patch", None),
        P("patch", None),
        P("patch", None),
        P(),
        P(),
        P(),
        P(),
        P(),
        P(),
        P(),
        P(None, "patch"),
        P(None, "patch"),
        P(),
        P("patch"),
        P("patch", None, None),
        P("patch"),
        P("patch"),
        P("patch"),
        P("patch"),
    )
    out_specs = P("mem", None, "patch")
    return jax.shard_map(
        per_device, mesh=mesh, in_specs=in_specs, out_specs=out_specs, check_vma=False
    )
```

```python
import functools

import jax
import jax.numpy as jnp
from jax import lax
from jax.experimental import pallas as pl
from jax.experimental.pallas import tpu as pltpu
from jax.sharding import PartitionSpec as P

epsilon = 1e-05
smooth = 0.25
f32, bf16 = jnp.float32, jnp.bfloat16
MESH = pl.DeviceIdType.MESH

LANES = 128
WIDTH = 512
NODES = 512
EDGES = 1024
DECODER = 1536
HALO = 96
SENT = 2 * HALO
TABLE = 256
POINTS = 512
CHANNELS = 87
PADDED = 96
MEMBERS = 8
Z_ROW = 8
PEERS = 3
CHUNKS = 2
CHUNK = POINTS // CHUNKS
EDGE_TILE = 512
GRID_TILE = 384
NODE_TILE = 256


def dot(a, b):
    return jnp.dot(a, b, preferred_element_type=f32)


def spread(row):
    return jnp.broadcast_to(row, (LANES, LANES)).T


def one_hot(rows, base, blocks):
    lanes = lax.broadcasted_iota(jnp.int32, rows.shape, 1)
    rows = rows.astype(jnp.int16)
    parts = [
        jnp.where(rows == (lanes + (base + LANES * b)).astype(jnp.int16), jnp.ones((), bf16), jnp.zeros((), bf16))
        for b in range(blocks)
    ]
    return parts[0] if blocks == 1 else jnp.concatenate(parts, 1)


def silu(v):
    half = (0.5 * v).astype(bf16)
    return half + half * jnp.tanh(half)


def inverse_spread(centred):
    return lax.rsqrt(jnp.mean(centred * centred, -1, keepdims=True) + epsilon)


def centre(weight):
    wide = weight.astype(f32)
    return (wide - jnp.mean(wide, -1, keepdims=True)).astype(bf16)


def slope(v):
    return v * lax.rsqrt(v * v + smooth * smooth)


def kernel(
    lat_h, elat_h, glat_h, ei_h, eo_h, ni_h, no_h, gi_h, go_h, ow_h, prior_h, target_h,
    cw_h, aw_h, sends_h, es_h, er_h, gs_h, count_h,
    out_ref,
    lat, elat, glat, ws, wr, wp, eo, ni, no, gws, gwe, node_part, go, ow, prior, target, cw, aw, sends, es, er, gs, count,
    chosen, halo, chosen_new, halo_new, table, from_halo, into_sent, grid_from_own, grid_from_halo, acc, acc_grid, live, message, updated, readout_weight, readout,
    diff, outgoing, incoming, beside, pairwise, partial, partial_in,
    load_sem, send_sem, recv_sem, send_new_sem, recv_new_sem, peer_sem, peer_in_sem, beside_sem, beside_in_sem,
    partial_sem, partial_in_sem,
):
    member = lax.axis_index("mem")
    band = lax.axis_index("patch")
    bands = lax.axis_size("patch")
    above = band + 1
    below = band - 1
    has_above = band < bands - 1
    has_below = band > 0
    sibling = member + 1 - 2 * lax.rem(member, 2)
    peers = [lax.rem(member + 2 * k, MEMBERS) for k in range(1, PEERS + 1)]

    loads = {}

    def load(name, source, target_ref):
        loads[name] = pltpu.make_async_copy(source, target_ref, load_sem.at[len(loads)])

    def begin(*names):
        for name in names:
            loads[name].start()

    def ready(*names):
        for name in names:
            loads[name].wait()

    load("sends", sends_h.at[0], sends)
    load("lat", lat_h.at[0], lat)
    load("ws", ei_h.at[pl.ds(0, WIDTH)], ws)
    load("wr", ei_h.at[pl.ds(WIDTH, WIDTH)], wr)
    load("es", es_h, es)
    load("er", er_h, er)
    load("count", count_h, count)
    load("we", ei_h.at[pl.ds(2 * WIDTH, WIDTH)], wp.at[pl.ds(0, WIDTH)])
    load("elat", elat_h, elat)
    load("eo", eo_h, eo)
    load("ni", ni_h, ni)
    load("no", no_h, no)
    load("gws", gi_h.at[pl.ds(0, WIDTH)], gws)
    load("gwe", gi_h.at[pl.ds(WIDTH, WIDTH)], gwe)
    load("gs", gs_h, gs)
    load("glat", glat_h, glat)
    load("go", go_h, go)
    load("ow", ow_h, ow)
    load("prior", prior_h, prior)
    load("target", target_h, target)
    load("cw", cw_h, cw)
    load("aw", aw_h, aw)
    begin("sends", "lat")
    barrier = pltpu.get_barrier_semaphore()

    def greet(other, row):
        pl.semaphore_signal(barrier, inc=1, device_id=(other, row), device_id_type=MESH)

    @pl.when(has_above)
    def _():
        greet(member, above)

    @pl.when(has_below)
    def _():
        greet(member, below)

    for other in peers + [sibling]:
        greet(other, band)

    begin("ws", "wr", "es", "er", "count")
    ready("sends")
    up = spread(jnp.concatenate([sends[0:1, :], jnp.zeros((1, LANES - HALO), jnp.int32)], 1))
    down = spread(jnp.concatenate([sends[1:2, :], jnp.zeros((1, LANES - HALO), jnp.int32)], 1))
    sent_rows = jnp.concatenate([up[:HALO], down[:HALO]], 0)
    for rows in (halo, halo_new):
        rows[SENT:, :] = jnp.zeros((TABLE - SENT, WIDTH), bf16)

        @pl.when(jnp.logical_not(has_below))
        def _():
            rows[:HALO, :] = jnp.zeros((HALO, WIDTH), bf16)

        @pl.when(jnp.logical_not(has_above))
        def _():
            rows[HALO:SENT, :] = jnp.zeros((HALO, WIDTH), bf16)

    ready("lat")
    begin("we", "elat")
    chosen[...] = dot(one_hot(sent_rows, 0, NODES // LANES), lat[...]).astype(bf16)

    def edge_rows(t, indices):
        each = EDGE_TILE // LANES
        return jnp.concatenate(
            [spread(indices[pl.ds(t * each + i, 1), :]) for i in range(each)], 0
        )

    def placing(nodes):
        blocks = [
            jnp.where(nodes == live[i : i + 1, :], 1.0, 0.0).astype(bf16)
            for i in range(EDGES // LANES)
        ]
        return jnp.concatenate(blocks, 1)

    def grid_rows(t):
        each = GRID_TILE // LANES
        return jnp.concatenate([spread(gs[pl.ds(t * each + i, 1), :]) for i in range(each)], 0)

    def edge_products():
        ready("ws", "wr", "es", "er", "count")
        wp[pl.ds(WIDTH, WIDTH), :] = dot(lat[...], ws[...]).astype(bf16)
        wp[pl.ds(2 * WIDTH, WIDTH), :] = dot(lat[...], wr[...]).astype(bf16)
        slots = (
            lax.broadcasted_iota(jnp.int32, (EDGES // LANES, LANES), 0) * LANES
            + lax.broadcasted_iota(jnp.int32, (EDGES // LANES, LANES), 1)
        )
        live[...] = jnp.where(slots < count[...], er[...], -1)
        ready("we", "elat")
        for t in range(EDGES // EDGE_TILE):
            rows = pl.ds(t * EDGE_TILE, EDGE_TILE)
            senders = edge_rows(t, es)
            from_halo[rows, :] = one_hot(senders, NODES, TABLE // LANES)
            picks = [
                elat[rows, :],
                one_hot(senders, 0, NODES // LANES),
                one_hot(edge_rows(t, er), 0, NODES // LANES),
            ]
            acc[rows, :] = dot(jnp.concatenate(picks, 1), wp[...])
        ready("eo")
        eo[...] = centre(eo[...])
        ready("ni", "no")
        no[...] = centre(no[...])
        into_sent[...] = placing(sent_rows)

    def decoder_products():
        ready("gwe", "gs", "glat")
        for t in range(DECODER // GRID_TILE):
            rows = pl.ds(t * GRID_TILE, GRID_TILE)
            senders = grid_rows(t)
            grid_from_own[rows, :] = one_hot(senders, 0, NODES // LANES)
            grid_from_halo[rows, :] = one_hot(senders, NODES, TABLE // LANES)
            acc_grid[rows, :] = dot(glat[rows, :], gwe[...])

    def begin_rest():
        begin("eo", "ni", "no", "gws", "gwe", "gs", "glat", "go", "ow", "prior", "target", "cw", "aw")

    ahead = lax.rem(band, Z_ROW) == 0

    @pl.when(ahead)
    def _():
        begin_rest()
        edge_products()
        decoder_products()

    pl.semaphore_wait(
        barrier, PEERS + 1 + has_above.astype(jnp.int32) + has_below.astype(jnp.int32)
    )

    def remote(source, into, send, recv, other, row):
        return pltpu.make_async_remote_copy(
            src_ref=source,
            dst_ref=into,
            send_sem=send,
            recv_sem=recv,
            device_id=(other, row),
            device_id_type=MESH,
        )

    def exchange(source, into, send, recv, i):
        there, neighbour = ((has_above, above), (has_below, below))[i]
        part = pl.ds(i * HALO, HALO)
        copy = remote(source.at[part], into.at[part], send.at[i], recv.at[i], member, neighbour)

        @pl.when(there)
        def _():
            copy.start()

        return copy

    def arrived(copies):
        for copy, there in zip(copies, (has_below, has_above)):

            @pl.when(there)
            def _():
                copy.wait_recv()

    def left(copies):
        for copy, there in zip(copies, (has_above, has_below)):

            @pl.when(there)
            def _():
                copy.wait_send()

    first = [exchange(chosen, halo, send_sem, recv_sem, i) for i in range(2)]

    @pl.when(jnp.logical_not(ahead))
    def _():
        begin_rest()
        edge_products()

    arrived(first)

    table[...] = dot(halo[...], ws[...]).astype(bf16)
    for t in range(EDGES // EDGE_TILE):
        rows = pl.ds(t * EDGE_TILE, EDGE_TILE)
        inner = silu(
            acc[rows, :] + dot(from_halo[rows, :], table[...])
        )
        outer = dot(inner, eo[...])
        message[rows, :] = (outer * inverse_spread(outer)).astype(bf16)


    def node_update(latent, placing):
        summed = dot(placing, message[...]).astype(bf16)
        inner = silu(dot(jnp.concatenate([latent, summed], 1), ni[...]))
        outer = dot(inner, no[...])
        return (latent.astype(f32) + outer * inverse_spread(outer)).astype(bf16)

    chosen_new[...] = node_update(chosen[...], into_sent[...])
    second = [exchange(chosen_new, halo_new, send_new_sem, recv_new_sem, 0)]

    for t in range(NODES // NODE_TILE):
        rows = pl.ds(t * NODE_TILE, NODE_TILE)
        nodes = lax.broadcasted_iota(jnp.int32, (NODE_TILE, LANES), 0) + t * NODE_TILE
        updated[rows, :] = node_update(lat[rows, :], placing(nodes))
        if t == 0:
            second.append(exchange(chosen_new, halo_new, send_new_sem, recv_new_sem, 1))

    @pl.when(jnp.logical_not(ahead))
    def _():
        decoder_products()

    ready("gws")
    node_part[...] = dot(updated[...], gws[...]).astype(bf16)
    for t in range(DECODER // GRID_TILE):
        rows = pl.ds(t * GRID_TILE, GRID_TILE)
        acc_grid[rows, :] += dot(grid_from_own[rows, :], node_part[...])
    ready("go", "ow", "prior", "target", "cw", "aw")
    go[...] = centre(go[...])
    readout_weight[...] = jnp.zeros_like(readout_weight)
    readout_weight[:, 0:CHANNELS] = ow[...].astype(f32).T.astype(bf16)
    arrived(second)

    table[...] = dot(halo_new[...], gws[...]).astype(bf16)
    diff[pl.ds(PADDED - 16, 16), :] = jnp.zeros((16, POINTS), f32)
    to_peers, to_sibling, to_partial = [], [], []
    for t in range(DECODER // GRID_TILE):
        rows = pl.ds(t * GRID_TILE, GRID_TILE)
        inner = silu(
            acc_grid[rows, :] + dot(grid_from_halo[rows, :], table[...])
        )
        outer = dot(inner, go[...])
        channels = dot(outer.astype(bf16), readout_weight[...])
        readout[rows, :] = channels * inverse_spread(outer)
        points = pl.ds(t * LANES, LANES)
        output = (
            readout[pl.ds(t * GRID_TILE, LANES, 3), :]
            + readout[pl.ds(t * GRID_TILE + 1, LANES, 3), :]
            + readout[pl.ds(t * GRID_TILE + 2, LANES, 3), :]
        )
        diff[0:CHANNELS, points] = (
            prior[:, points] + output.T[0:CHANNELS] - target[:, points]
        )
        chunk, part = divmod(t * LANES, CHUNK)
        outgoing[chunk, :, pl.ds(part, LANES)] = diff[:, points].astype(bf16)
        if part + LANES == CHUNK:
            to_peers.append([
                remote(
                    outgoing.at[chunk], incoming.at[chunk, k], peer_sem.at[chunk, k],
                    peer_in_sem.at[chunk, k], peers[k], band,
                )
                for k in (1, 0, 2)
            ])
            to_sibling.append(
                remote(
                    outgoing.at[chunk], beside.at[chunk], beside_sem.at[chunk],
                    beside_in_sem.at[chunk], sibling, band,
                )
            )

            @pl.when(band >= 0)
            def _():
                for copy in to_peers[-1] + to_sibling[-1:]:
                    copy.start()


    gains = spread(
        jnp.concatenate([cw[...], jnp.zeros((1, LANES - CHANNELS), f32)], 1)
    )
    blocks = [pl.ds(part, LANES) for part in range(0, CHUNK, LANES)]
    for chunk in range(CHUNKS):
        to_sibling[chunk].wait_recv()
        for copy in to_peers[chunk]:
            copy.wait_recv()
        for block in blocks:
            near = beside[chunk, :, block].astype(f32)
            total = None
            for k in range(PEERS):
                term = slope(near - incoming[chunk, k, :, block].astype(f32))
                total = term if total is None else total + term
            partial[chunk, :, block] = total.astype(bf16)
        copy = remote(
            partial.at[chunk], partial_in.at[chunk], partial_sem.at[chunk],
            partial_in_sem.at[chunk], sibling, band,
        )
        copy.start()
        to_partial.append(copy)
        for block in blocks:
            points = pl.ds(chunk * CHUNK + block.start, LANES)
            own = diff[:, points]
            total = slope(own - beside[chunk, :, block].astype(f32))
            for k in range(PEERS):
                total = total + slope(own - incoming[chunk, k, :, block].astype(f32))
            pairwise[:, points] = slope(own) - total * (1.0 / (MEMBERS - 1))
    for chunk in range(CHUNKS):
        to_partial[chunk].wait_recv()
        for block in blocks:
            points = pl.ds(chunk * CHUNK + block.start, LANES)
            t = (chunk * CHUNK + block.start) // LANES
            result = pairwise[:, points] - partial_in[chunk, :, block].astype(f32) * (
                1.0 / (MEMBERS - 1)
            )
            result = result * gains[:PADDED] * aw[t : t + 1, :]
            out_ref[0, :, points] = result[0:CHANNELS]
    left(first)
    left(second)
    for chunk in range(CHUNKS):
        for copy in to_peers[chunk] + [to_sibling[chunk], to_partial[chunk]]:
            copy.wait_send()


def per_device(
    mesh_latent, edge_latent, grid_edge_latent, edge_inner, edge_outer, node_inner, node_outer,
    grid_inner, grid_outer, out_weight, prior_state, target, channel_weight, area_weight,
    send_rows, edge_senders, edge_receivers, edge_count, grid_senders,
):
    hbm = pl.BlockSpec(memory_space=pltpu.HBM)
    dma = pltpu.SemaphoreType.DMA
    vmem = pltpu.VMEM
    square = vmem((WIDTH, WIDTH), bf16)
    scratch = [
        square,
        vmem((EDGES, WIDTH), bf16),
        vmem((DECODER, WIDTH), bf16),
        square,
        square,
        vmem((3 * WIDTH, WIDTH), bf16),
        square,
        vmem((2 * WIDTH, WIDTH), bf16),
        square,
        square,
        square,
        square,
        square,
        vmem((CHANNELS, WIDTH), bf16),
        vmem((CHANNELS, POINTS), f32),
        vmem((CHANNELS, POINTS), f32),
        vmem((1, CHANNELS), f32),
        vmem((POINTS // LANES, LANES), f32),
        vmem((2, HALO), jnp.int32),
        vmem((EDGES // LANES, LANES), jnp.int32),
        vmem((EDGES // LANES, LANES), jnp.int32),
        vmem((DECODER // LANES, LANES), jnp.int32),
        vmem((1, 1), jnp.int32),
        vmem((SENT, WIDTH), bf16),
        vmem((TABLE, WIDTH), bf16),
        vmem((SENT, WIDTH), bf16),
        vmem((TABLE, WIDTH), bf16),
        vmem((TABLE, WIDTH), bf16),
        vmem((EDGES, TABLE), bf16),
        vmem((SENT, EDGES), bf16),
        vmem((DECODER, NODES), bf16),
        vmem((DECODER, TABLE), bf16),
        vmem((EDGES, WIDTH), f32),
        vmem((DECODER, WIDTH), f32),
        vmem((EDGES // LANES, LANES), jnp.int32),
        vmem((EDGES, WIDTH), bf16),
        vmem((NODES, WIDTH), bf16),
        vmem((WIDTH, LANES), bf16),
        vmem((DECODER, LANES), f32),
        vmem((PADDED, POINTS), f32),
        vmem((CHUNKS, PADDED, CHUNK), bf16),
        vmem((CHUNKS, PEERS, PADDED, CHUNK), bf16),
        vmem((CHUNKS, PADDED, CHUNK), bf16),
        vmem((PADDED, POINTS), f32),
        vmem((CHUNKS, PADDED, CHUNK), bf16),
        vmem((CHUNKS, PADDED, CHUNK), bf16),
        dma((22,)),
        dma((2,)),
        dma((2,)),
        dma((2,)),
        dma((2,)),
        dma((CHUNKS, PEERS)),
        dma((CHUNKS, PEERS)),
        dma((CHUNKS,)),
        dma((CHUNKS,)),
        dma((CHUNKS,)),
        dma((CHUNKS,)),
    ]
    return pl.pallas_call(
        kernel,
        out_shape=pltpu.VMEM((1, CHANNELS, POINTS), f32),
        in_specs=[hbm] * 19,
        out_specs=pl.BlockSpec(memory_space=pltpu.VMEM),
        scratch_shapes=scratch,
        compiler_params=pltpu.CompilerParams(
            collective_id=0, has_side_effects=True, vmem_limit_bytes=60 * 1024 * 1024
        ),
        cost_estimate=pl.CostEstimate(
            flops=9_000_000_000, bytes_accessed=9_000_000, transcendentals=2_000_000
        ),
        name="ensemble_layers",
    )(
        mesh_latent, edge_latent, grid_edge_latent, edge_inner, edge_outer, node_inner, node_outer,
        grid_inner, grid_outer, out_weight, prior_state, target,
        channel_weight.reshape(1, CHANNELS),
        area_weight.reshape(POINTS // LANES, LANES),
        send_rows,
        edge_senders.reshape(EDGES // LANES, LANES),
        edge_receivers.reshape(EDGES // LANES, LANES),
        grid_senders.reshape(DECODER // LANES, LANES),
        edge_count.reshape(1, 1),
    )


def solution(mesh):
    in_specs = (
        P("mem", "patch", None),
        P("patch", None),
        P("patch", None),
        P(),
        P(),
        P(),
        P(),
        P(),
        P(),
        P(),
        P(None, "patch"),
        P(None, "patch"),
        P(),
        P("patch"),
        P("patch", None, None),
        P("patch"),
        P("patch"),
        P("patch"),
        P("patch"),
    )
    out_specs = P("mem", None, "patch")
    return jax.shard_map(
        per_device, mesh=mesh, in_specs=in_specs, out_specs=out_specs, check_vma=False
    )
```

```python
import functools

import jax
import jax.numpy as jnp
from jax import lax
from jax.experimental import pallas as pl
from jax.experimental.pallas import tpu as pltpu
from jax.sharding import PartitionSpec as P

epsilon = 1e-05
smooth = 0.25
f32, bf16 = jnp.float32, jnp.bfloat16
MESH = pl.DeviceIdType.MESH

LANES = 128
WIDTH = 512
NODES = 512
EDGES = 1024
DECODER = 1536
HALO = 96
SENT = 2 * HALO
TABLE = 256
POINTS = 512
CHANNELS = 87
PADDED = 96
MEMBERS = 8
Z_ROW = 8
PEERS = 3
CHUNKS = 2
CHUNK = POINTS // CHUNKS
EDGE_TILE = 512
GRID_TILE = 384
NODE_TILE = 256


def dot(a, b):
    return jnp.dot(a, b, preferred_element_type=f32)


def spread(row):
    return jnp.broadcast_to(row, (LANES, LANES)).T


def one_hot(rows, base, blocks):
    lanes = lax.broadcasted_iota(jnp.int32, rows.shape, 1)
    rows = rows.astype(jnp.int16)
    parts = [
        jnp.where(rows == (lanes + (base + LANES * b)).astype(jnp.int16), jnp.ones((), bf16), jnp.zeros((), bf16))
        for b in range(blocks)
    ]
    return parts[0] if blocks == 1 else jnp.concatenate(parts, 1)


def silu(v):
    half = (0.5 * v).astype(bf16)
    return half + half * jnp.tanh(half)


def inverse_spread(centred):
    return lax.rsqrt(jnp.mean(centred * centred, -1, keepdims=True) + epsilon)


def centre(weight):
    wide = weight.astype(f32)
    return (wide - jnp.mean(wide, -1, keepdims=True)).astype(bf16)


def slope(v):
    return v * lax.rsqrt(v * v + smooth * smooth)


def kernel(
    lat_h, elat_h, glat_h, ei_h, eo_h, ni_h, no_h, gi_h, go_h, ow_h, prior_h, target_h,
    cw_h, aw_h, sends_h, es_h, er_h, gs_h, count_h,
    out_ref,
    lat, elat, glat, ws, wr, wp, eo, ni, no, gws, gwe, node_part, go, ow, prior, target, cw, aw, sends, es, er, gs, count,
    chosen, halo, chosen_new, halo_new, table, from_halo, into_sent, grid_from_own, grid_from_halo, acc, acc_grid, live, message, updated, readout_weight, readout,
    diff, outgoing, incoming, beside, pairwise, partial, partial_in,
    load_sem, send_sem, recv_sem, send_new_sem, recv_new_sem, peer_sem, peer_in_sem, beside_sem, beside_in_sem,
    partial_sem, partial_in_sem,
):
    member = lax.axis_index("mem")
    band = lax.axis_index("patch")
    bands = lax.axis_size("patch")
    above = band + 1
    below = band - 1
    has_above = band < bands - 1
    has_below = band > 0
    sibling = member + 1 - 2 * lax.rem(member, 2)
    peers = [lax.rem(member + 2 * k, MEMBERS) for k in range(1, PEERS + 1)]

    loads = {}

    def load(name, source, target_ref):
        loads[name] = pltpu.make_async_copy(source, target_ref, load_sem.at[len(loads)])

    def begin(*names):
        for name in names:
            loads[name].start()

    def ready(*names):
        for name in names:
            loads[name].wait()

    load("sends", sends_h.at[0], sends)
    load("lat", lat_h.at[0], lat)
    load("ws", ei_h.at[pl.ds(0, WIDTH)], ws)
    load("wr", ei_h.at[pl.ds(WIDTH, WIDTH)], wr)
    load("es", es_h, es)
    load("er", er_h, er)
    load("count", count_h, count)
    load("we", ei_h.at[pl.ds(2 * WIDTH, WIDTH)], wp.at[pl.ds(0, WIDTH)])
    load("elat", elat_h, elat)
    load("eo", eo_h, eo)
    load("ni", ni_h, ni)
    load("no", no_h, no)
    load("gws", gi_h.at[pl.ds(0, WIDTH)], gws)
    load("gwe", gi_h.at[pl.ds(WIDTH, WIDTH)], gwe)
    load("gs", gs_h, gs)
    load("glat", glat_h, glat)
    load("go", go_h, go)
    load("ow", ow_h, ow)
    load("prior", prior_h, prior)
    load("target", target_h, target)
    load("cw", cw_h, cw)
    load("aw", aw_h, aw)
    begin("sends", "lat")
    barrier = pltpu.get_barrier_semaphore()

    def greet(other, row):
        pl.semaphore_signal(barrier, inc=1, device_id=(other, row), device_id_type=MESH)

    @pl.when(has_above)
    def _():
        greet(member, above)

    @pl.when(has_below)
    def _():
        greet(member, below)

    for other in peers + [sibling]:
        greet(other, band)

    begin("ws", "wr", "es", "er", "count")
    ready("sends")
    up = spread(jnp.concatenate([sends[0:1, :], jnp.zeros((1, LANES - HALO), jnp.int32)], 1))
    down = spread(jnp.concatenate([sends[1:2, :], jnp.zeros((1, LANES - HALO), jnp.int32)], 1))
    sent_rows = jnp.concatenate([up[:HALO], down[:HALO]], 0)
    for rows in (halo, halo_new):
        rows[SENT:, :] = jnp.zeros((TABLE - SENT, WIDTH), bf16)

        @pl.when(jnp.logical_not(has_below))
        def _():
            rows[:HALO, :] = jnp.zeros((HALO, WIDTH), bf16)

        @pl.when(jnp.logical_not(has_above))
        def _():
            rows[HALO:SENT, :] = jnp.zeros((HALO, WIDTH), bf16)

    ready("lat")
    begin("we", "elat")
    chosen[...] = dot(one_hot(sent_rows, 0, NODES // LANES), lat[...]).astype(bf16)

    def edge_rows(t, indices):
        each = EDGE_TILE // LANES
        return jnp.concatenate(
            [spread(indices[pl.ds(t * each + i, 1), :]) for i in range(each)], 0
        )

    def placing(nodes):
        blocks = [
            jnp.where(nodes == live[i : i + 1, :], 1.0, 0.0).astype(bf16)
            for i in range(EDGES // LANES)
        ]
        return jnp.concatenate(blocks, 1)

    def grid_rows(t):
        each = GRID_TILE // LANES
        return jnp.concatenate([spread(gs[pl.ds(t * each + i, 1), :]) for i in range(each)], 0)

    def edge_products():
        ready("ws", "wr", "es", "er", "count")
        wp[pl.ds(WIDTH, WIDTH), :] = dot(lat[...], ws[...]).astype(bf16)
        wp[pl.ds(2 * WIDTH, WIDTH), :] = dot(lat[...], wr[...]).astype(bf16)
        slots = (
            lax.broadcasted_iota(jnp.int32, (EDGES // LANES, LANES), 0) * LANES
            + lax.broadcasted_iota(jnp.int32, (EDGES // LANES, LANES), 1)
        )
        live[...] = jnp.where(slots < count[...], er[...], -1)
        ready("we", "elat")
        for t in range(EDGES // EDGE_TILE):
            if t == EDGES // EDGE_TILE - 1:
                ready("eo", "ni", "no")
                into_sent[...] = placing(sent_rows)
                eo[...] = centre(eo[...])
                no[...] = centre(no[...])
            rows = pl.ds(t * EDGE_TILE, EDGE_TILE)
            senders = edge_rows(t, es)
            from_halo[rows, :] = one_hot(senders, NODES, TABLE // LANES)
            picks = [
                elat[rows, :],
                one_hot(senders, 0, NODES // LANES),
                one_hot(edge_rows(t, er), 0, NODES // LANES),
            ]
            acc[rows, :] = dot(jnp.concatenate(picks, 1), wp[...])

    def decoder_products():
        ready("gwe", "gs", "glat")
        for t in range(DECODER // GRID_TILE):
            rows = pl.ds(t * GRID_TILE, GRID_TILE)
            senders = grid_rows(t)
            grid_from_own[rows, :] = one_hot(senders, 0, NODES // LANES)
            grid_from_halo[rows, :] = one_hot(senders, NODES, TABLE // LANES)
            acc_grid[rows, :] = dot(glat[rows, :], gwe[...])

    def begin_rest():
        begin("eo", "ni", "no", "gws", "gwe", "gs", "glat", "go", "ow", "prior", "target", "cw", "aw")

    ahead = lax.rem(band, Z_ROW) == 0

    @pl.when(ahead)
    def _():
        begin_rest()
        edge_products()
        decoder_products()

    pl.semaphore_wait(
        barrier, PEERS + 1 + has_above.astype(jnp.int32) + has_below.astype(jnp.int32)
    )

    def remote(source, into, send, recv, other, row):
        return pltpu.make_async_remote_copy(
            src_ref=source,
            dst_ref=into,
            send_sem=send,
            recv_sem=recv,
            device_id=(other, row),
            device_id_type=MESH,
        )

    def exchange(source, into, send, recv, i):
        there, neighbour = ((has_above, above), (has_below, below))[i]
        part = pl.ds(i * HALO, HALO)
        copy = remote(source.at[part], into.at[part], send.at[i], recv.at[i], member, neighbour)

        @pl.when(there)
        def _():
            copy.start()

        return copy

    def arrived(copies):
        for copy, there in zip(copies, (has_below, has_above)):

            @pl.when(there)
            def _():
                copy.wait_recv()

    def left(copies):
        for copy, there in zip(copies, (has_above, has_below)):

            @pl.when(there)
            def _():
                copy.wait_send()

    first = [exchange(chosen, halo, send_sem, recv_sem, i) for i in range(2)]

    @pl.when(jnp.logical_not(ahead))
    def _():
        begin_rest()
        edge_products()

    arrived(first)

    table[...] = dot(halo[...], ws[...]).astype(bf16)
    for t in range(EDGES // EDGE_TILE):
        rows = pl.ds(t * EDGE_TILE, EDGE_TILE)
        inner = silu(
            acc[rows, :] + dot(from_halo[rows, :], table[...])
        )
        outer = dot(inner, eo[...])
        message[rows, :] = (outer * inverse_spread(outer)).astype(bf16)


    def node_update(latent, placing):
        summed = dot(placing, message[...]).astype(bf16)
        inner = silu(dot(jnp.concatenate([latent, summed], 1), ni[...]))
        outer = dot(inner, no[...])
        return (latent.astype(f32) + outer * inverse_spread(outer)).astype(bf16)

    chosen_new[...] = node_update(chosen[...], into_sent[...])
    second = [exchange(chosen_new, halo_new, send_new_sem, recv_new_sem, 0)]

    for t in range(NODES // NODE_TILE):
        rows = pl.ds(t * NODE_TILE, NODE_TILE)
        nodes = lax.broadcasted_iota(jnp.int32, (NODE_TILE, LANES), 0) + t * NODE_TILE
        updated[rows, :] = node_update(lat[rows, :], placing(nodes))
        if t == 0:
            second.append(exchange(chosen_new, halo_new, send_new_sem, recv_new_sem, 1))

    @pl.when(jnp.logical_not(ahead))
    def _():
        decoder_products()

    ready("gws")
    ready("go", "ow", "prior", "target", "cw", "aw")
    go[...] = centre(go[...])
    readout_weight[...] = jnp.zeros_like(readout_weight)
    readout_weight[:, 0:CHANNELS] = ow[...].astype(f32).T.astype(bf16)
    node_part[...] = dot(updated[...], gws[...]).astype(bf16)
    for t in range(DECODER // GRID_TILE):
        rows = pl.ds(t * GRID_TILE, GRID_TILE)
        acc_grid[rows, :] += dot(grid_from_own[rows, :], node_part[...])
    arrived(second)

    table[...] = dot(halo_new[...], gws[...]).astype(bf16)
    diff[pl.ds(PADDED - 16, 16), :] = jnp.zeros((16, POINTS), f32)
    to_peers, to_sibling, to_partial = [], [], []
    for t in range(DECODER // GRID_TILE):
        rows = pl.ds(t * GRID_TILE, GRID_TILE)
        inner = silu(
            acc_grid[rows, :] + dot(grid_from_halo[rows, :], table[...])
        )
        outer = dot(inner, go[...])
        channels = dot(outer.astype(bf16), readout_weight[...])
        readout[rows, :] = channels * inverse_spread(outer)
        points = pl.ds(t * LANES, LANES)
        output = (
            readout[pl.ds(t * GRID_TILE, LANES, 3), :]
            + readout[pl.ds(t * GRID_TILE + 1, LANES, 3), :]
            + readout[pl.ds(t * GRID_TILE + 2, LANES, 3), :]
        )
        diff[0:CHANNELS, points] = (
            prior[:, points] + output.T[0:CHANNELS] - target[:, points]
        )
        chunk, part = divmod(t * LANES, CHUNK)
        outgoing[chunk, :, pl.ds(part, LANES)] = diff[:, points].astype(bf16)
        if part + LANES == CHUNK:
            to_peers.append([
                remote(
                    outgoing.at[chunk], incoming.at[chunk, k], peer_sem.at[chunk, k],
                    peer_in_sem.at[chunk, k], peers[k], band,
                )
                for k in (1, 0, 2)
            ])
            to_sibling.append(
                remote(
                    outgoing.at[chunk], beside.at[chunk], beside_sem.at[chunk],
                    beside_in_sem.at[chunk], sibling, band,
                )
            )

            @pl.when(band >= 0)
            def _():
                for copy in to_peers[-1] + to_sibling[-1:]:
                    copy.start()


    gains = spread(
        jnp.concatenate([cw[...], jnp.zeros((1, LANES - CHANNELS), f32)], 1)
    )
    blocks = [pl.ds(part, LANES) for part in range(0, CHUNK, LANES)]
    for chunk in range(CHUNKS):
        to_sibling[chunk].wait_recv()
        for copy in to_peers[chunk]:
            copy.wait_recv()
        for block in blocks:
            near = beside[chunk, :, block].astype(f32)
            total = None
            for k in range(PEERS):
                term = slope(near - incoming[chunk, k, :, block].astype(f32))
                total = term if total is None else total + term
            partial[chunk, :, block] = total.astype(bf16)
        copy = remote(
            partial.at[chunk], partial_in.at[chunk], partial_sem.at[chunk],
            partial_in_sem.at[chunk], sibling, band,
        )
        copy.start()
        to_partial.append(copy)
        for block in blocks:
            points = pl.ds(chunk * CHUNK + block.start, LANES)
            own = diff[:, points]
            total = slope(own - beside[chunk, :, block].astype(f32))
            for k in range(PEERS):
                total = total + slope(own - incoming[chunk, k, :, block].astype(f32))
            pairwise[:, points] = slope(own) - total * (1.0 / (MEMBERS - 1))
    for chunk in range(CHUNKS):
        to_partial[chunk].wait_recv()
        for block in blocks:
            points = pl.ds(chunk * CHUNK + block.start, LANES)
            t = (chunk * CHUNK + block.start) // LANES
            result = pairwise[:, points] - partial_in[chunk, :, block].astype(f32) * (
                1.0 / (MEMBERS - 1)
            )
            result = result * gains[:PADDED] * aw[t : t + 1, :]
            out_ref[0, :, points] = result[0:CHANNELS]
    left(first)
    left(second)
    for chunk in range(CHUNKS):
        for copy in to_peers[chunk] + [to_sibling[chunk], to_partial[chunk]]:
            copy.wait_send()


def per_device(
    mesh_latent, edge_latent, grid_edge_latent, edge_inner, edge_outer, node_inner, node_outer,
    grid_inner, grid_outer, out_weight, prior_state, target, channel_weight, area_weight,
    send_rows, edge_senders, edge_receivers, edge_count, grid_senders,
):
    hbm = pl.BlockSpec(memory_space=pltpu.HBM)
    dma = pltpu.SemaphoreType.DMA
    vmem = pltpu.VMEM
    square = vmem((WIDTH, WIDTH), bf16)
    scratch = [
        square,
        vmem((EDGES, WIDTH), bf16),
        vmem((DECODER, WIDTH), bf16),
        square,
        square,
        vmem((3 * WIDTH, WIDTH), bf16),
        square,
        vmem((2 * WIDTH, WIDTH), bf16),
        square,
        square,
        square,
        square,
        square,
        vmem((CHANNELS, WIDTH), bf16),
        vmem((CHANNELS, POINTS), f32),
        vmem((CHANNELS, POINTS), f32),
        vmem((1, CHANNELS), f32),
        vmem((POINTS // LANES, LANES), f32),
        vmem((2, HALO), jnp.int32),
        vmem((EDGES // LANES, LANES), jnp.int32),
        vmem((EDGES // LANES, LANES), jnp.int32),
        vmem((DECODER // LANES, LANES), jnp.int32),
        vmem((1, 1), jnp.int32),
        vmem((SENT, WIDTH), bf16),
        vmem((TABLE, WIDTH), bf16),
        vmem((SENT, WIDTH), bf16),
        vmem((TABLE, WIDTH), bf16),
        vmem((TABLE, WIDTH), bf16),
        vmem((EDGES, TABLE), bf16),
        vmem((SENT, EDGES), bf16),
        vmem((DECODER, NODES), bf16),
        vmem((DECODER, TABLE), bf16),
        vmem((EDGES, WIDTH), f32),
        vmem((DECODER, WIDTH), f32),
        vmem((EDGES // LANES, LANES), jnp.int32),
        vmem((EDGES, WIDTH), bf16),
        vmem((NODES, WIDTH), bf16),
        vmem((WIDTH, LANES), bf16),
        vmem((DECODER, LANES), f32),
        vmem((PADDED, POINTS), f32),
        vmem((CHUNKS, PADDED, CHUNK), bf16),
        vmem((CHUNKS, PEERS, PADDED, CHUNK), bf16),
        vmem((CHUNKS, PADDED, CHUNK), bf16),
        vmem((PADDED, POINTS), f32),
        vmem((CHUNKS, PADDED, CHUNK), bf16),
        vmem((CHUNKS, PADDED, CHUNK), bf16),
        dma((22,)),
        dma((2,)),
        dma((2,)),
        dma((2,)),
        dma((2,)),
        dma((CHUNKS, PEERS)),
        dma((CHUNKS, PEERS)),
        dma((CHUNKS,)),
        dma((CHUNKS,)),
        dma((CHUNKS,)),
        dma((CHUNKS,)),
    ]
    return pl.pallas_call(
        kernel,
        out_shape=pltpu.VMEM((1, CHANNELS, POINTS), f32),
        in_specs=[hbm] * 19,
        out_specs=pl.BlockSpec(memory_space=pltpu.VMEM),
        scratch_shapes=scratch,
        compiler_params=pltpu.CompilerParams(
            collective_id=0, has_side_effects=True, vmem_limit_bytes=60 * 1024 * 1024
        ),
        cost_estimate=pl.CostEstimate(
            flops=9_000_000_000, bytes_accessed=9_000_000, transcendentals=2_000_000
        ),
        name="ensemble_layers",
    )(
        mesh_latent, edge_latent, grid_edge_latent, edge_inner, edge_outer, node_inner, node_outer,
        grid_inner, grid_outer, out_weight, prior_state, target,
        channel_weight.reshape(1, CHANNELS),
        area_weight.reshape(POINTS // LANES, LANES),
        send_rows,
        edge_senders.reshape(EDGES // LANES, LANES),
        edge_receivers.reshape(EDGES // LANES, LANES),
        grid_senders.reshape(DECODER // LANES, LANES),
        edge_count.reshape(1, 1),
    )


def solution(mesh):
    in_specs = (
        P("mem", "patch", None),
        P("patch", None),
        P("patch", None),
        P(),
        P(),
        P(),
        P(),
        P(),
        P(),
        P(),
        P(None, "patch"),
        P(None, "patch"),
        P(),
        P("patch"),
        P("patch", None, None),
        P("patch"),
        P("patch"),
        P("patch"),
        P("patch"),
    )
    out_specs = P("mem", None, "patch")
    return jax.shard_map(
        per_device, mesh=mesh, in_specs=in_specs, out_specs=out_specs, check_vma=False
    )
```

```python
import functools

import jax
import jax.numpy as jnp
from jax import lax
from jax.experimental import pallas as pl
from jax.experimental.pallas import tpu as pltpu
from jax.sharding import PartitionSpec as P

epsilon = 1e-05
smooth = 0.25
f32, bf16 = jnp.float32, jnp.bfloat16
MESH = pl.DeviceIdType.MESH

LANES = 128
WIDTH = 512
NODES = 512
EDGES = 1024
DECODER = 1536
HALO = 96
SENT = 2 * HALO
TABLE = 256
POINTS = 512
CHANNELS = 87
PADDED = 96
MEMBERS = 8
Z_ROW = 8
PEERS = 3
CHUNKS = 2
CHUNK = POINTS // CHUNKS
EDGE_TILE = 512
GRID_TILE = 384
NODE_TILE = 512


def dot(a, b):
    return jnp.dot(a, b, preferred_element_type=f32)


def spread(row):
    return jnp.broadcast_to(row, (LANES, LANES)).T


def one_hot(rows, base, blocks):
    lanes = lax.broadcasted_iota(jnp.int32, rows.shape, 1)
    rows = rows.astype(jnp.int16)
    parts = [
        jnp.where(rows == (lanes + (base + LANES * b)).astype(jnp.int16), jnp.ones((), bf16), jnp.zeros((), bf16))
        for b in range(blocks)
    ]
    return parts[0] if blocks == 1 else jnp.concatenate(parts, 1)


def silu(v):
    half = (0.5 * v).astype(bf16)
    return half + half * jnp.tanh(half)


def inverse_spread(centred):
    return lax.rsqrt(jnp.mean(centred * centred, -1, keepdims=True) + epsilon)


def centre(weight):
    wide = weight.astype(f32)
    return (wide - jnp.mean(wide, -1, keepdims=True)).astype(bf16)


def slope(v):
    return v * lax.rsqrt(v * v + smooth * smooth)


def kernel(
    lat_h, elat_h, glat_h, ei_h, eo_h, ni_h, no_h, gi_h, go_h, ow_h, prior_h, target_h,
    cw_h, aw_h, sends_h, es_h, er_h, gs_h, count_h,
    out_ref,
    lat, elat, glat, ws, wr, wp, eo, ni, no, gws, gwe, node_part, go, ow, prior, target, cw, aw, sends, es, er, gs, count,
    chosen, halo, chosen_new, halo_new, table, from_halo, into_sent, grid_from_own, grid_from_halo, acc, acc_grid, live, message, updated, readout_weight, readout,
    diff, outgoing, incoming, beside, pairwise, partial, partial_in,
    load_sem, send_sem, recv_sem, send_new_sem, recv_new_sem, peer_sem, peer_in_sem, beside_sem, beside_in_sem,
    partial_sem, partial_in_sem,
):
    member = lax.axis_index("mem")
    band = lax.axis_index("patch")
    bands = lax.axis_size("patch")
    above = band + 1
    below = band - 1
    has_above = band < bands - 1
    has_below = band > 0
    sibling = member + 1 - 2 * lax.rem(member, 2)
    peers = [lax.rem(member + 2 * k, MEMBERS) for k in range(1, PEERS + 1)]

    loads = {}

    def load(name, source, target_ref):
        loads[name] = pltpu.make_async_copy(source, target_ref, load_sem.at[len(loads)])

    def begin(*names):
        for name in names:
            loads[name].start()

    def ready(*names):
        for name in names:
            loads[name].wait()

    load("sends", sends_h.at[0], sends)
    load("lat", lat_h.at[0], lat)
    load("ws", ei_h.at[pl.ds(0, WIDTH)], ws)
    load("wr", ei_h.at[pl.ds(WIDTH, WIDTH)], wr)
    load("es", es_h, es)
    load("er", er_h, er)
    load("count", count_h, count)
    load("we", ei_h.at[pl.ds(2 * WIDTH, WIDTH)], wp.at[pl.ds(0, WIDTH)])
    load("elat", elat_h, elat)
    load("eo", eo_h, eo)
    load("ni", ni_h, ni)
    load("no", no_h, no)
    load("gws", gi_h.at[pl.ds(0, WIDTH)], gws)
    load("gwe", gi_h.at[pl.ds(WIDTH, WIDTH)], gwe)
    load("gs", gs_h, gs)
    load("glat", glat_h, glat)
    load("go", go_h, go)
    load("ow", ow_h, ow)
    load("prior", prior_h, prior)
    load("target", target_h, target)
    load("cw", cw_h, cw)
    load("aw", aw_h, aw)
    begin("sends", "lat")
    barrier = pltpu.get_barrier_semaphore()

    def greet(other, row):
        pl.semaphore_signal(barrier, inc=1, device_id=(other, row), device_id_type=MESH)

    @pl.when(has_above)
    def _():
        greet(member, above)

    @pl.when(has_below)
    def _():
        greet(member, below)

    for other in peers + [sibling]:
        greet(other, band)

    begin("ws", "wr", "es", "er", "count")
    ready("sends")
    up = spread(jnp.concatenate([sends[0:1, :], jnp.zeros((1, LANES - HALO), jnp.int32)], 1))
    down = spread(jnp.concatenate([sends[1:2, :], jnp.zeros((1, LANES - HALO), jnp.int32)], 1))
    sent_rows = jnp.concatenate([up[:HALO], down[:HALO]], 0)
    for rows in (halo, halo_new):
        rows[SENT:, :] = jnp.zeros((TABLE - SENT, WIDTH), bf16)

        @pl.when(jnp.logical_not(has_below))
        def _():
            rows[:HALO, :] = jnp.zeros((HALO, WIDTH), bf16)

        @pl.when(jnp.logical_not(has_above))
        def _():
            rows[HALO:SENT, :] = jnp.zeros((HALO, WIDTH), bf16)

    ready("lat")
    begin("we", "elat")
    chosen[...] = dot(one_hot(sent_rows, 0, NODES // LANES), lat[...]).astype(bf16)

    def edge_rows(t, indices):
        each = EDGE_TILE // LANES
        return jnp.concatenate(
            [spread(indices[pl.ds(t * each + i, 1), :]) for i in range(each)], 0
        )

    def placing(nodes):
        blocks = [
            jnp.where(nodes == live[i : i + 1, :], 1.0, 0.0).astype(bf16)
            for i in range(EDGES // LANES)
        ]
        return jnp.concatenate(blocks, 1)

    def grid_rows(t):
        each = GRID_TILE // LANES
        return jnp.concatenate([spread(gs[pl.ds(t * each + i, 1), :]) for i in range(each)], 0)

    def edge_products():
        ready("ws", "wr", "es", "er", "count")
        wp[pl.ds(WIDTH, WIDTH), :] = dot(lat[...], ws[...]).astype(bf16)
        wp[pl.ds(2 * WIDTH, WIDTH), :] = dot(lat[...], wr[...]).astype(bf16)
        slots = (
            lax.broadcasted_iota(jnp.int32, (EDGES // LANES, LANES), 0) * LANES
            + lax.broadcasted_iota(jnp.int32, (EDGES // LANES, LANES), 1)
        )
        live[...] = jnp.where(slots < count[...], er[...], -1)
        ready("we", "elat")
        for t in range(EDGES // EDGE_TILE):
            if t == EDGES // EDGE_TILE - 1:
                ready("eo", "ni", "no")
                into_sent[...] = placing(sent_rows)
                eo[...] = centre(eo[...])
                no[...] = centre(no[...])
            rows = pl.ds(t * EDGE_TILE, EDGE_TILE)
            senders = edge_rows(t, es)
            from_halo[rows, :] = one_hot(senders, NODES, TABLE // LANES)
            picks = [
                elat[rows, :],
                one_hot(senders, 0, NODES // LANES),
                one_hot(edge_rows(t, er), 0, NODES // LANES),
            ]
            acc[rows, :] = dot(jnp.concatenate(picks, 1), wp[...])

    def decoder_products():
        ready("gwe", "gs", "glat")
        for t in range(DECODER // GRID_TILE):
            rows = pl.ds(t * GRID_TILE, GRID_TILE)
            senders = grid_rows(t)
            grid_from_own[rows, :] = one_hot(senders, 0, NODES // LANES)
            grid_from_halo[rows, :] = one_hot(senders, NODES, TABLE // LANES)
            acc_grid[rows, :] = dot(glat[rows, :], gwe[...])

    def begin_rest():
        begin("eo", "ni", "no", "gws", "gwe", "gs", "glat", "go", "ow", "prior", "target", "cw", "aw")

    ahead = lax.rem(band, Z_ROW) == 0

    @pl.when(ahead)
    def _():
        begin_rest()
        edge_products()
        decoder_products()

    pl.semaphore_wait(
        barrier, PEERS + 1 + has_above.astype(jnp.int32) + has_below.astype(jnp.int32)
    )

    def remote(source, into, send, recv, other, row):
        return pltpu.make_async_remote_copy(
            src_ref=source,
            dst_ref=into,
            send_sem=send,
            recv_sem=recv,
            device_id=(other, row),
            device_id_type=MESH,
        )

    def exchange(source, into, send, recv, i):
        there, neighbour = ((has_above, above), (has_below, below))[i]
        part = pl.ds(i * HALO, HALO)
        copy = remote(source.at[part], into.at[part], send.at[i], recv.at[i], member, neighbour)

        @pl.when(there)
        def _():
            copy.start()

        return copy

    def arrived(copies):
        for copy, there in zip(copies, (has_below, has_above)):

            @pl.when(there)
            def _():
                copy.wait_recv()

    def left(copies):
        for copy, there in zip(copies, (has_above, has_below)):

            @pl.when(there)
            def _():
                copy.wait_send()

    first = [exchange(chosen, halo, send_sem, recv_sem, i) for i in range(2)]

    @pl.when(jnp.logical_not(ahead))
    def _():
        begin_rest()
        edge_products()

    arrived(first)

    table[...] = dot(halo[...], ws[...]).astype(bf16)
    for t in range(EDGES // EDGE_TILE):
        rows = pl.ds(t * EDGE_TILE, EDGE_TILE)
        inner = silu(
            acc[rows, :] + dot(from_halo[rows, :], table[...])
        )
        outer = dot(inner, eo[...])
        message[rows, :] = (outer * inverse_spread(outer)).astype(bf16)


    def node_update(latent, placing):
        summed = dot(placing, message[...]).astype(bf16)
        inner = silu(dot(jnp.concatenate([latent, summed], 1), ni[...]))
        outer = dot(inner, no[...])
        return (latent.astype(f32) + outer * inverse_spread(outer)).astype(bf16)

    chosen_new[...] = node_update(chosen[...], into_sent[...])
    second = [exchange(chosen_new, halo_new, send_new_sem, recv_new_sem, i) for i in range(2)]

    for t in range(NODES // NODE_TILE):
        rows = pl.ds(t * NODE_TILE, NODE_TILE)
        nodes = lax.broadcasted_iota(jnp.int32, (NODE_TILE, LANES), 0) + t * NODE_TILE
        updated[rows, :] = node_update(lat[rows, :], placing(nodes))

    @pl.when(jnp.logical_not(ahead))
    def _():
        decoder_products()

    ready("gws")
    ready("go", "ow", "prior", "target", "cw", "aw")
    go[...] = centre(go[...])
    readout_weight[...] = jnp.zeros_like(readout_weight)
    readout_weight[:, 0:CHANNELS] = ow[...].astype(f32).T.astype(bf16)
    node_part[...] = dot(updated[...], gws[...]).astype(bf16)
    for t in range(DECODER // GRID_TILE):
        rows = pl.ds(t * GRID_TILE, GRID_TILE)
        acc_grid[rows, :] += dot(grid_from_own[rows, :], node_part[...])
    arrived(second)

    table[...] = dot(halo_new[...], gws[...]).astype(bf16)
    diff[pl.ds(PADDED - 16, 16), :] = jnp.zeros((16, POINTS), f32)
    to_peers, to_sibling, to_partial = [], [], []
    for t in range(DECODER // GRID_TILE):
        rows = pl.ds(t * GRID_TILE, GRID_TILE)
        inner = silu(
            acc_grid[rows, :] + dot(grid_from_halo[rows, :], table[...])
        )
        outer = dot(inner, go[...])
        channels = dot(outer.astype(bf16), readout_weight[...])
        readout[rows, :] = channels * inverse_spread(outer)
        points = pl.ds(t * LANES, LANES)
        output = (
            readout[pl.ds(t * GRID_TILE, LANES, 3), :]
            + readout[pl.ds(t * GRID_TILE + 1, LANES, 3), :]
            + readout[pl.ds(t * GRID_TILE + 2, LANES, 3), :]
        )
        diff[0:CHANNELS, points] = (
            prior[:, points] + output.T[0:CHANNELS] - target[:, points]
        )
        chunk, part = divmod(t * LANES, CHUNK)
        outgoing[chunk, :, pl.ds(part, LANES)] = diff[:, points].astype(bf16)
        if part + LANES == CHUNK:
            to_peers.append([
                remote(
                    outgoing.at[chunk], incoming.at[chunk, k], peer_sem.at[chunk, k],
                    peer_in_sem.at[chunk, k], peers[k], band,
                )
                for k in (1, 0, 2)
            ])
            to_sibling.append(
                remote(
                    outgoing.at[chunk], beside.at[chunk], beside_sem.at[chunk],
                    beside_in_sem.at[chunk], sibling, band,
                )
            )

            @pl.when(band >= 0)
            def _():
                for copy in to_peers[-1] + to_sibling[-1:]:
                    copy.start()


    gains = spread(
        jnp.concatenate([cw[...], jnp.zeros((1, LANES - CHANNELS), f32)], 1)
    )
    blocks = [pl.ds(part, LANES) for part in range(0, CHUNK, LANES)]
    for chunk in range(CHUNKS):
        to_sibling[chunk].wait_recv()
        for copy in to_peers[chunk]:
            copy.wait_recv()
        for block in blocks:
            near = beside[chunk, :, block].astype(f32)
            total = None
            for k in range(PEERS):
                term = slope(near - incoming[chunk, k, :, block].astype(f32))
                total = term if total is None else total + term
            partial[chunk, :, block] = total.astype(bf16)
        copy = remote(
            partial.at[chunk], partial_in.at[chunk], partial_sem.at[chunk],
            partial_in_sem.at[chunk], sibling, band,
        )
        copy.start()
        to_partial.append(copy)
        for block in blocks:
            points = pl.ds(chunk * CHUNK + block.start, LANES)
            own = diff[:, points]
            total = slope(own - beside[chunk, :, block].astype(f32))
            for k in range(PEERS):
                total = total + slope(own - incoming[chunk, k, :, block].astype(f32))
            pairwise[:, points] = slope(own) - total * (1.0 / (MEMBERS - 1))
    for chunk in range(CHUNKS):
        to_partial[chunk].wait_recv()
        for block in blocks:
            points = pl.ds(chunk * CHUNK + block.start, LANES)
            t = (chunk * CHUNK + block.start) // LANES
            result = pairwise[:, points] - partial_in[chunk, :, block].astype(f32) * (
                1.0 / (MEMBERS - 1)
            )
            result = result * gains[:PADDED] * aw[t : t + 1, :]
            out_ref[0, :, points] = result[0:CHANNELS]
    left(first)
    left(second)
    for chunk in range(CHUNKS):
        for copy in to_peers[chunk] + [to_sibling[chunk], to_partial[chunk]]:
            copy.wait_send()


def per_device(
    mesh_latent, edge_latent, grid_edge_latent, edge_inner, edge_outer, node_inner, node_outer,
    grid_inner, grid_outer, out_weight, prior_state, target, channel_weight, area_weight,
    send_rows, edge_senders, edge_receivers, edge_count, grid_senders,
):
    hbm = pl.BlockSpec(memory_space=pltpu.HBM)
    dma = pltpu.SemaphoreType.DMA
    vmem = pltpu.VMEM
    square = vmem((WIDTH, WIDTH), bf16)
    scratch = [
        square,
        vmem((EDGES, WIDTH), bf16),
        vmem((DECODER, WIDTH), bf16),
        square,
        square,
        vmem((3 * WIDTH, WIDTH), bf16),
        square,
        vmem((2 * WIDTH, WIDTH), bf16),
        square,
        square,
        square,
        square,
        square,
        vmem((CHANNELS, WIDTH), bf16),
        vmem((CHANNELS, POINTS), f32),
        vmem((CHANNELS, POINTS), f32),
        vmem((1, CHANNELS), f32),
        vmem((POINTS // LANES, LANES), f32),
        vmem((2, HALO), jnp.int32),
        vmem((EDGES // LANES, LANES), jnp.int32),
        vmem((EDGES // LANES, LANES), jnp.int32),
        vmem((DECODER // LANES, LANES), jnp.int32),
        vmem((1, 1), jnp.int32),
        vmem((SENT, WIDTH), bf16),
        vmem((TABLE, WIDTH), bf16),
        vmem((SENT, WIDTH), bf16),
        vmem((TABLE, WIDTH), bf16),
        vmem((TABLE, WIDTH), bf16),
        vmem((EDGES, TABLE), bf16),
        vmem((SENT, EDGES), bf16),
        vmem((DECODER, NODES), bf16),
        vmem((DECODER, TABLE), bf16),
        vmem((EDGES, WIDTH), f32),
        vmem((DECODER, WIDTH), f32),
        vmem((EDGES // LANES, LANES), jnp.int32),
        vmem((EDGES, WIDTH), bf16),
        vmem((NODES, WIDTH), bf16),
        vmem((WIDTH, LANES), bf16),
        vmem((DECODER, LANES), f32),
        vmem((PADDED, POINTS), f32),
        vmem((CHUNKS, PADDED, CHUNK), bf16),
        vmem((CHUNKS, PEERS, PADDED, CHUNK), bf16),
        vmem((CHUNKS, PADDED, CHUNK), bf16),
        vmem((PADDED, POINTS), f32),
        vmem((CHUNKS, PADDED, CHUNK), bf16),
        vmem((CHUNKS, PADDED, CHUNK), bf16),
        dma((22,)),
        dma((2,)),
        dma((2,)),
        dma((2,)),
        dma((2,)),
        dma((CHUNKS, PEERS)),
        dma((CHUNKS, PEERS)),
        dma((CHUNKS,)),
        dma((CHUNKS,)),
        dma((CHUNKS,)),
        dma((CHUNKS,)),
    ]
    return pl.pallas_call(
        kernel,
        out_shape=pltpu.VMEM((1, CHANNELS, POINTS), f32),
        in_specs=[hbm] * 19,
        out_specs=pl.BlockSpec(memory_space=pltpu.VMEM),
        scratch_shapes=scratch,
        compiler_params=pltpu.CompilerParams(
            collective_id=0, has_side_effects=True, vmem_limit_bytes=60 * 1024 * 1024
        ),
        cost_estimate=pl.CostEstimate(
            flops=9_000_000_000, bytes_accessed=9_000_000, transcendentals=2_000_000
        ),
        name="ensemble_layers",
    )(
        mesh_latent, edge_latent, grid_edge_latent, edge_inner, edge_outer, node_inner, node_outer,
        grid_inner, grid_outer, out_weight, prior_state, target,
        channel_weight.reshape(1, CHANNELS),
        area_weight.reshape(POINTS // LANES, LANES),
        send_rows,
        edge_senders.reshape(EDGES // LANES, LANES),
        edge_receivers.reshape(EDGES // LANES, LANES),
        grid_senders.reshape(DECODER // LANES, LANES),
        edge_count.reshape(1, 1),
    )


def solution(mesh):
    in_specs = (
        P("mem", "patch", None),
        P("patch", None),
        P("patch", None),
        P(),
        P(),
        P(),
        P(),
        P(),
        P(),
        P(),
        P(None, "patch"),
        P(None, "patch"),
        P(),
        P("patch"),
        P("patch", None, None),
        P("patch"),
        P("patch"),
        P("patch"),
        P("patch"),
    )
    out_specs = P("mem", None, "patch")
    return jax.shard_map(
        per_device, mesh=mesh, in_specs=in_specs, out_specs=out_specs, check_vma=False
    )
```
